32 devices in a mesh: tile: 8 (over z, x), pass: 4 (over y, core).
Axes of the slice: x: 2, y: 2, z: 4, core: 2. Of those that a mesh axis runs over, the one named last changes fastest.
Arguments:
- obs_local: float32 [2, 3, 32768], P(None, None, ('tile', 'pass')), may hold values from -0.2 to 1.2
- obs_value: float32 [32768], P(('tile', 'pass')), may hold values from -6 to 6
- obs_weight: float32 [32768], P(('tile', 'pass')), may hold values from 0.5 to 8
- seg_tiles: int32 [512, 2], P(('tile', 'pass')), may hold values from 0 to 7, all different within a row; in each aligned block of 16 rows (0 to 15, 16 to 31, ...) at most 4 rows name the same one
- comp_scale: int32 [1024], P('tile'), may hold values from 0 to 3
- comp_orient: int32 [1024], P('tile'), may hold values from 0 to 7
- comp_place: int32 [1024], P('tile'), may hold values from 0 to 511
Outputs:
- coefficients: float32 [1024], P('tile')
- grid_field: float32 [8, 4, 1024], P('tile', 'pass')
The draws below stay inside these ranges and needn't reach their ends.
Inputs may be any that keep to these rules, and one draw needn't show every extreme that they name: `seg_tiles`: each row names 2 different tiles. Among the rows of one device no tile is named by more than 4 rows, a bound that some block reaches.
All inputs are finite; a program needn't handle non-finite values.
Results may differ from the reference program's by a relative error of at most 0.0003.
Values sent between devices are 32-bit elements; how exact they have to be, the bound alone decides.
A program may use at most 64 MiB of HBM per device.

```python
import math
import jax
import jax.numpy as jnp
import numpy as np
from jax import lax

K = 128
SEGS_DEV = 16
SEG = 64
TOP = 2
ITERS = 2
GX = 32
GY = 32
MOST = 4
SEGS = 512
OBS = 32768
COMPS = 1024
DAYS = 4
N_TILE = 8


def set_ends(result, key, least, top_value):
    shape = result.shape
    index_at = [jax.random.randint(jax.random.fold_in(key, axis), (), 0, shape[axis]) for axis in range(len(shape))]
    result = result.at[tuple(index_at)].set(least)
    longest = shape.index(max(shape))
    index_at[longest] = (index_at[longest] + 1) % shape[longest]
    return result.at[tuple(index_at)].set(top_value)


def block_levels(rng, dims, pieces, smallest, high):
    def one(dim, blocks):
        steps = jax.random.uniform(jax.random.fold_in(jax.random.fold_in(rng, 6), dim), (blocks,), jnp.float32, smallest / len(pieces), high / len(pieces))
        return jnp.repeat(jnp.exp(steps), dims[dim] // blocks).reshape((-1,) + (1,) * (len(dims) - dim - 1))

    loudness = one(*pieces[0])
    for cut in pieces[1:]:
        loudness = loudness * one(*cut)
    return loudness


def routed_block(stream_key, own, number, rows, number_of, top, most, skew):
    ranking = jax.random.permutation(stream_key, number_of)
    packed, usual = portions_of(number_of, rows * top, most, skew, True), portions_of(number_of, rows * top, most, skew, False)
    places = jnp.arange(number_of)

    def named(tallies, offset_by):
        used = int((tallies > 0).sum())
        fixed = max(1, used // 4)
        moved = fixed + (places - fixed + offset_by * (used - fixed)) % max(1, number_of - fixed)
        return jnp.zeros((number_of,), jnp.int32).at[ranking[jnp.where(places < fixed, places, moved)]].set(jnp.asarray(tallies, jnp.int32))

    tallies = jnp.where(number % 4 == 0, named(packed, number // 4), named(usual, number - number // 4 - 1))
    mixed = jax.random.permutation(jax.random.fold_in(own, 3), number_of)
    donor, receiver = mixed[0:number_of // 2 * 2:2], mixed[1:number_of // 2 * 2:2]
    slack = jnp.minimum(tallies[donor] - 1, most - tallies[receiver]) // 2
    slack = jnp.where((donor == ranking[0]) | (receiver == ranking[0]) | (tallies[receiver] == 0), 0, jnp.maximum(slack, 0))
    moved = jax.random.randint(jax.random.fold_in(own, 4), (number_of // 2,), 0, 1 << 20) % (slack + 1)
    tallies = tallies.at[donor].add(-moved).at[receiver].add(moved)
    items = jnp.searchsorted(jnp.cumsum(tallies), jnp.arange(rows * top), side="right").astype(jnp.int32)
    grid = items.reshape(top, rows).T
    grid = grid[jax.random.permutation(jax.random.fold_in(own, 1), rows)]
    offset_by = jax.random.randint(jax.random.fold_in(own, 2), (rows, 1), 0, top)
    return jnp.take_along_axis(grid, (jnp.arange(top)[None, :] + offset_by) % top, axis=1)


def portions_of(amount, total, limit, lean, full):
    portions = [(1 << 20) // math.isqrt(standing ** lean) + 1 for standing in range(1, amount + 1)]
    largest = limit if full else min(limit, max(-(-total // amount), total * portions[0] // sum(portions)))
    least = 1 if total - largest >= amount - 1 else 0
    counts, surplus = [largest] + [least] * (amount - 1), total - largest - least * (amount - 1)
    while surplus > 0:
        movable = [i for i in range(1, amount) if counts[i] < largest] or [i for i in range(1, amount) if counts[i] < limit]
        whole, budget = sum([portions[i] for i in movable]), surplus
        for i in movable:
            more = min(limit - counts[i], max(1, budget * portions[i] // whole), surplus)
            counts[i] = counts[i] + more
            surplus = surplus - more
    return np.array(counts)


def bell_draw(own_key, dims, spread, reach, pieces=(), kind=jnp.bfloat16):
    array = jax.random.normal(own_key, dims, jnp.float32) * spread
    if len(pieces) > 0:
        array = block_levels(own_key, dims, pieces, -0.22, 0.18) * array
    return jnp.clip(array, min=-reach, max=reach).astype(kind)


def setup_inputs(seed: int = 0) -> dict:
    key_of = jax.random.split(jax.random.key(seed), 8)
    obs_local = jnp.clip(-0.2 + 1.4000001 * jax.random.uniform(key_of[0], (TOP, 3, OBS), jnp.float32) ** block_levels(key_of[0], (TOP, 3, OBS), ((2, 32),), -0.2, 0.2), -0.2, 1.2)
    obs_value = bell_draw(key_of[1], (OBS,), 1.0, 6.0, ((0, 32),), jnp.float32)
    obs_weight = jnp.clip(jnp.exp(math.log(8.0) - 2.7725887 * jax.random.uniform(key_of[2], (OBS,), jnp.float32) ** block_levels(key_of[2], (OBS,), ((0, 32),), -0.2, 0.2)), 0.5, 8.0)
    seg_tiles_keys = jax.random.split(jax.random.fold_in(key_of[3], 1), SEGS // SEGS_DEV)
    seg_tiles_turns = jax.random.permutation(jax.random.fold_in(key_of[3], 3), SEGS // SEGS_DEV)
    seg_tiles = jax.vmap(lambda own, number: routed_block(jax.random.fold_in(key_of[3], 2), own, number, SEGS_DEV, N_TILE, TOP, MOST, 2))(seg_tiles_keys, seg_tiles_turns).reshape((SEGS, TOP))
    comp_scale = set_ends(jax.random.randint(key_of[4], (COMPS,), 0, 4), jax.random.fold_in(key_of[4], 1), 0, 3).astype(jnp.int32)
    comp_orient = set_ends(jax.random.randint(key_of[5], (COMPS,), 0, 8), jax.random.fold_in(key_of[5], 1), 0, 7).astype(jnp.int32)
    comp_place = set_ends(jax.random.randint(key_of[6], (COMPS,), 0, 512), jax.random.fold_in(key_of[6], 1), 0, 511).astype(jnp.int32)
    return {"obs_local": obs_local, "obs_value": obs_value, "obs_weight": obs_weight, "seg_tiles": seg_tiles, "comp_scale": comp_scale, "comp_orient": comp_orient, "comp_place": comp_place}


TIME_RATE = 8.0
HIGHEST = lax.Precision.HIGHEST


def wavelet_table(scale_index, orient_index, place_index):
    level = scale_index.astype(jnp.float32)
    width = 0.4 * jnp.power(0.7, level)
    wave_number = 2.2 / width
    angle = math.pi * orient_index.astype(jnp.float32) / 8.0
    center_x = ((place_index % 8).astype(jnp.float32) + 0.5) / 8.0
    center_y = (((place_index // 8) % 8).astype(jnp.float32) + 0.5) / 8.0
    center_t = ((place_index // 64).astype(jnp.float32) + 0.5) / 8.0
    return jnp.stack([center_x, center_y, center_t, 0.5 / (width * width),
                      wave_number * jnp.cos(angle), wave_number * jnp.sin(angle)])


def gabor_value(delta_x, delta_y, delta_t, inverse_width, wave_x, wave_y):
    envelope = jnp.exp(-(delta_x * delta_x + delta_y * delta_y) * inverse_width - TIME_RATE * delta_t * delta_t)
    return envelope * jnp.cos(delta_x * wave_x + delta_y * wave_y)


def route_basis(position, params):
    delta_x = position[0][:, :, None] - params[0][:, None, :]
    delta_y = position[1][:, :, None] - params[1][:, None, :]
    delta_t = position[2][:, :, None] - params[2][:, None, :]
    return gabor_value(delta_x, delta_y, delta_t, params[3][:, None, :], params[4][:, None, :], params[5][:, None, :])


def grid_basis(place_x, place_y, day_time, params, offset):
    delta_x = place_x[None, :, None] - (params[0] + offset)[None, None, :]
    delta_y = place_y[None, :, None] - params[1][None, None, :]
    delta_t = day_time[:, None, None] - params[2][None, None, :]
    return gabor_value(delta_x, delta_y, delta_t, params[3][None, None, :], params[4][None, None, :], params[5][None, None, :])


def reference(obs_local, obs_value, obs_weight, seg_tiles, comp_scale, comp_orient, comp_place):
    wavelets = wavelet_table(comp_scale, comp_orient, comp_place)
    tile_count = comp_scale.shape[0] // K
    tile_wavelets = wavelets.reshape(6, tile_count, K)
    prior_weight = 2.0 * jnp.power(1.5, comp_scale.astype(jnp.float32))
    seg_count = seg_tiles.shape[0]
    block_count = seg_count // SEGS_DEV
    positions = obs_local.reshape(TOP, 3, block_count, SEGS_DEV, SEG).transpose(2, 0, 1, 3, 4)
    block_tiles = seg_tiles.reshape(block_count, SEGS_DEV, TOP)
    weights = obs_weight.reshape(seg_count, SEG)
    weighted_value = weights * obs_value.reshape(seg_count, SEG)

    def forward(direction):
        direction_tiles = direction.reshape(tile_count, K)

        def evaluate_block(inputs):
            position, tile_ids = inputs
            values = jnp.zeros((SEGS_DEV, SEG), jnp.float32)
            for route in range(TOP):
                params = jnp.take(tile_wavelets, tile_ids[:, route], axis=1)
                basis = route_basis(position[route], params)
                values = values + jnp.einsum("sjk,sk->sj", basis, direction_tiles[tile_ids[:, route]], precision=HIGHEST)
            return values

        return lax.map(evaluate_block, (positions, block_tiles)).reshape(seg_count, SEG)

    def adjoint(values):
        value_blocks = values.reshape(block_count, SEGS_DEV, SEG)

        def accumulate(running, inputs):
            position, tile_ids, value = inputs
            for route in range(TOP):
                params = jnp.take(tile_wavelets, tile_ids[:, route], axis=1)
                basis = route_basis(position[route], params)
                running = running.at[tile_ids[:, route]].add(jnp.einsum("sjk,sj->sk", basis, value, precision=HIGHEST))
            return running, None

        running, _ = lax.scan(accumulate, jnp.zeros((tile_count, K), jnp.float32), (positions, block_tiles, value_blocks))
        return running.reshape(-1)

    def normal_apply(direction):
        return adjoint(weights * forward(direction)) + prior_weight * direction

    rhs = adjoint(weighted_value)
    coefficients = jnp.zeros_like(rhs)
    residual = rhs
    direction = rhs
    norm_now = jnp.sum(residual * residual)
    for iteration in range(ITERS):
        image = normal_apply(direction)
        step_size = norm_now / jnp.sum(direction * image)
        coefficients = coefficients + step_size * direction
        residual = residual - step_size * image
        norm_next = jnp.sum(residual * residual)
        direction = residual + (norm_next / norm_now) * direction
        norm_now = norm_next

    cell_x = (jnp.arange(GX, dtype=jnp.float32) + 0.5) / GX
    cell_y = (jnp.arange(GY, dtype=jnp.float32) + 0.5) / GY
    place_x = jnp.repeat(cell_x, GY)
    place_y = jnp.tile(cell_y, GX)
    day_time = (jnp.arange(DAYS, dtype=jnp.float32) + 0.5) / DAYS
    coefficient_tiles = coefficients.reshape(tile_count, K)

    def tile_field(tile):
        field = jnp.zeros((DAYS, GX * GY), jnp.float32)
        for offset in (-1, 0, 1):
            neighbor = (tile + offset) % tile_count
            params = jnp.take(tile_wavelets, neighbor, axis=1)
            basis = grid_basis(place_x, place_y, day_time, params, offset)
            field = field + jnp.einsum("dgk,k->dg", basis, jnp.take(coefficient_tiles, neighbor, axis=0), precision=HIGHEST)
        return field

    grid_field = lax.map(tile_field, jnp.arange(tile_count, dtype=jnp.int32))
    return coefficients, grid_field
```

```python
import functools
import math

import jax
import jax.numpy as jnp
import numpy as np
from jax import lax
from jax.experimental import pallas as pl
from jax.experimental.pallas import tpu as pltpu
from jax.sharding import PartitionSpec as P

GX = 32
GY = 32
LANES = 128
TIME_RATE = 8.0
LOG2E = math.log2(math.e)
TIME_SCALE = math.sqrt(TIME_RATE * LOG2E)
ROUNDER = 12582912.0
HIGHEST = lax.Precision.HIGHEST
MESH = pl.DeviceIdType.MESH


def cosine_polynomial(degree):
    fit = np.polynomial.Chebyshev.interpolate(
        lambda z: np.cos(2 * np.pi * np.sqrt(np.maximum(z, 0.0))), degree, domain=[0.0, 0.25]
    )
    return [float(c) for c in fit.convert(kind=np.polynomial.Polynomial).coef]


COSINE = cosine_polynomial(6)


def cos_turns(turns):
    part = turns - jnp.round(turns)
    square = part * part
    total = jnp.full_like(square, COSINE[-1])
    for coefficient in COSINE[-2::-1]:
        total = total * square + coefficient
    return total


def peers(count, body):
    if count <= 8:
        for distance in range(1, count):
            body(distance)
    else:

        def step(distance, carry):
            body(distance)
            return carry

        lax.fori_loop(1, count, step, 0)


def total_of(value):
    return jnp.sum(jnp.sum(value, axis=1, keepdims=True), axis=0, keepdims=True)


def kernel(
    tiles, passes, obs_ref, value_ref, weight_ref, seg_ref, scale_ref, orient_ref, place_ref,
    coef_ref, field_ref,
    table, stack, columns, basis, vectors, grid_x, grid_y,
    near, far, last_near, last_far, table_sems, near_sems, far_sems,
):
    my_tile, my_pass = lax.axis_index("tile"), lax.axis_index("pass")
    seg_count, fan_out = seg_ref.shape
    points = value_ref.shape[1]
    seg_length = points // seg_count

    barrier = pltpu.get_barrier_semaphore()
    peers(passes, lambda d: pl.semaphore_signal(
        barrier, inc=1, device_id={"pass": lax.rem(my_pass + d, passes)}, device_id_type=MESH))
    peers(tiles, lambda d: pl.semaphore_signal(
        barrier, inc=1, device_id={"tile": lax.rem(my_tile + d, tiles)}, device_id_type=MESH))

    def to_peer(buffer, axis, me, count, sems, distance):
        return pltpu.make_async_remote_copy(
            src_ref=buffer.at[me],
            dst_ref=buffer.at[me],
            send_sem=sems.at[0, distance],
            recv_sem=sems.at[1, distance],
            device_id={axis: lax.rem(me + distance, count)},
            device_id_type=MESH,
        )

    level = scale_ref[...].astype(jnp.float32)
    width = 0.4 * jnp.exp(level * math.log(0.7))
    wave = 2.2 / (2.0 * math.pi) / width
    turns = orient_ref[...].astype(jnp.float32) / 16.0
    place = place_ref[...]
    table[my_tile, 0:1, :] = ((place & 7).astype(jnp.float32) + 0.5) / 8.0
    table[my_tile, 1:2, :] = (((place >> 3) & 7).astype(jnp.float32) + 0.5) / 8.0
    table[my_tile, 2:3, :] = ((place >> 6).astype(jnp.float32) + 0.5) * (TIME_SCALE / 8.0)
    table[my_tile, 3:4, :] = 0.5 * LOG2E / (width * width)
    table[my_tile, 4:5, :] = wave * cos_turns(turns)
    table[my_tile, 5:6, :] = wave * cos_turns(turns - 0.25)
    table[my_tile, 6:7, :] = 2.0 * jnp.exp(level * math.log(1.5))
    table[my_tile, 7:8, :] = jnp.zeros((1, LANES), jnp.float32)

    pl.semaphore_wait(barrier, passes + tiles - 2)
    peers(tiles, lambda d: to_peer(table, "tile", my_tile, tiles, table_sems, d).start())

    weights = weight_ref[...]
    for route in range(fan_out):
        stack[3 * route : 3 * route + 2, :] = obs_ref[route, 0:2, :]
        stack[3 * route + 2 : 3 * route + 3, :] = obs_ref[route, 2:3, :] * TIME_SCALE
    stack[3 * fan_out : 3 * fan_out + 1, :] = weights
    stack[3 * fan_out + 1 : 3 * fan_out + 2, :] = weights * value_ref[...]
    for start in range(0, points, LANES):
        columns[start : start + LANES, :] = stack[:, start : start + LANES].T

    def column(seg, which):
        rows = pl.ds(pl.multiple_of(seg * seg_length, seg_length), seg_length)
        return jnp.broadcast_to(columns[rows, which : which + 1], (seg_length, LANES))

    peers(tiles, lambda d: to_peer(table, "tile", my_tile, tiles, table_sems, d).wait_recv())

    tile_row = lax.broadcasted_iota(jnp.int32, (tiles, LANES), 0)

    def gather_into(running, tile, block):
        part = jnp.sum(block, axis=0, keepdims=True)
        return running + jnp.where(tile_row == tile, part, 0.0)

    def build(seg, running):
        weighted = column(seg, 3 * fan_out + 1)
        for route in range(fan_out):
            tile = seg_ref[seg, route]
            param = lambda row: table[tile, row : row + 1, :]
            delta_x = column(seg, 3 * route) - param(0)
            delta_y = column(seg, 3 * route + 1) - param(1)
            delta_t = column(seg, 3 * route + 2) - param(2)
            envelope = jnp.exp2(
                -(delta_x * delta_x + delta_y * delta_y) * param(3) - delta_t * delta_t
            )
            phi = envelope * cos_turns(delta_x * param(4) + delta_y * param(5))
            basis[seg * fan_out + route] = phi
            running = gather_into(running, tile, phi * weighted)
        return running

    def forward(which, seg):
        total = jnp.zeros((seg_length, LANES), jnp.float32)
        for route in range(fan_out):
            tile = seg_ref[seg, route]
            total = total + basis[seg * fan_out + route] * vectors[which, pl.ds(tile, 1), :]
        return jnp.sum(total, axis=1, keepdims=True)

    def normal(seg, running):
        weighted = forward(0, seg) * column(seg, 3 * fan_out)
        for route in range(fan_out):
            running = gather_into(
                running, seg_ref[seg, route], basis[seg * fan_out + route] * weighted
            )
        return running

    def energy(seg, running):
        values = forward(1, seg)
        return running + values * values * column(seg, 3 * fan_out)

    def sum_slots(buffer, count):
        if count <= 8:
            total = buffer[0]
            for slot in range(1, count):
                total = total + buffer[slot]
            return total
        return lax.fori_loop(1, count, lambda slot, total: total + buffer[slot], buffer[0])

    def all_sum(value, near_slots, far_slots, near_sem, far_sem, beside=None):
        near_slots[my_pass] = value
        peers(passes, lambda d: to_peer(near_slots, "pass", my_pass, passes, near_sem, d).start())
        if beside is not None:
            beside[0]()
        peers(passes, lambda d: to_peer(near_slots, "pass", my_pass, passes, near_sem, d).wait_recv())
        far_slots[my_tile] = sum_slots(near_slots, passes)
        peers(tiles, lambda d: to_peer(far_slots, "tile", my_tile, tiles, far_sem, d).start())
        if beside is not None:
            beside[1]()
        peers(tiles, lambda d: to_peer(far_slots, "tile", my_tile, tiles, far_sem, d).wait_recv())
        return sum_slots(far_slots, tiles)

    def grid_params(neighbor):
        tile = lax.rem(my_tile + (neighbor - 1) + tiles, tiles)
        return tile, lambda row: table[tile, row : row + 1, :]

    def axis_factors(delta, inverse, wave_row):
        envelope = jnp.exp2(-(delta * delta) * inverse)
        phase = delta * wave_row
        return envelope * cos_turns(phase), envelope * cos_turns(phase - 0.25)

    def grid_factors_y():
        cell = lax.broadcasted_iota(jnp.int32, (LANES, LANES), 0) & (GY - 1)
        place_y = (cell.astype(jnp.float32) + 0.5) / GY
        for neighbor in range(3):
            _, param = grid_params(neighbor)
            even, odd = axis_factors(place_y - param(1), param(3), param(5))
            grid_y[neighbor, :, :LANES] = even
            grid_y[neighbor, :, LANES:] = odd

    def grid_factors_x():
        row = lax.broadcasted_iota(jnp.int32, (GX, LANES), 0)
        cell = (row & 7) * (GX // 8) + (row >> 3)
        place_x = (cell.astype(jnp.float32) + 0.5) / GX
        day = (my_pass.astype(jnp.float32) + 0.5) / passes * TIME_SCALE
        for neighbor in range(3):
            _, param = grid_params(neighbor)
            even, odd = axis_factors(
                place_x - (param(0) + float(neighbor - 1)), param(3), param(4)
            )
            delta_t = day - param(2)
            in_time = jnp.exp2(-(delta_t * delta_t))
            grid_x[neighbor, :, :LANES] = even * in_time
            grid_x[neighbor, :, LANES:] = -odd * in_time

    zeros = jnp.zeros((tiles, LANES), jnp.float32)
    rhs = all_sum(
        lax.fori_loop(0, seg_count, build, zeros),
        near.at[0], far.at[0], near_sems.at[0], far_sems.at[0],
        (grid_factors_x, grid_factors_y),
    )
    norm_first = total_of(rhs * rhs)
    prior = table[:, 6, :]
    vectors[0] = rhs
    image = all_sum(
        lax.fori_loop(0, seg_count, normal, zeros),
        near.at[1], far.at[1], near_sems.at[1], far_sems.at[1],
    ) + prior * rhs
    step_first = norm_first / total_of(rhs * image)
    residual = rhs - step_first * image
    norm_next = total_of(residual * residual)
    direction = residual + norm_next / norm_first * rhs
    vectors[1] = direction

    fields = []

    def grid_fields():
        total = None
        for neighbor in range(3):
            tile, _ = grid_params(neighbor)
            parts = []
            for which in range(2):
                row = vectors[which, pl.ds(tile, 1), :]
                parts.append(grid_x[neighbor] * jnp.concatenate([row, row], axis=1))
            term = lax.dot_general(
                jnp.concatenate(parts, axis=0),
                grid_y[neighbor],
                (((1,), (1,)), ((), ())),
                precision=HIGHEST,
                preferred_element_type=jnp.float32,
            )
            total = term if total is None else total + term
        group = lax.broadcasted_iota(jnp.int32, (8, LANES), 1) // GY
        for begin in (0, GX):
            field = jnp.zeros((8, LANES), jnp.float32)
            for part in range(GX // 8):
                field = field + jnp.where(
                    group == part, total[begin + 8 * part : begin + 8 * part + 8, :], 0.0
                )
            fields.append(field)

    energies = lax.fori_loop(
        0, seg_count, energy, jnp.zeros((seg_length, LANES), jnp.float32)
    )
    folded = jnp.sum(energies, axis=0, keepdims=True)
    product = all_sum(
        folded, last_near, last_far, near_sems.at[2], far_sems.at[2],
        (grid_fields, lambda: None),
    )[:, 0:1] + total_of(direction * direction * prior)
    step_second = norm_next / product
    mine = pl.ds(my_tile, 1)
    coef_ref[...] = step_first * vectors[0, mine, :] + step_second * vectors[1, mine, :]
    field_ref[...] = step_first * fields[0] + step_second * fields[1]

    peers(tiles, lambda d: to_peer(table, "tile", my_tile, tiles, table_sems, d).wait_send())
    for stage in range(3):
        near_slots = near.at[stage] if stage < 2 else last_near
        far_slots = far.at[stage] if stage < 2 else last_far
        peers(passes, lambda d: to_peer(
            near_slots, "pass", my_pass, passes, near_sems.at[stage], d).wait_send())
        peers(tiles, lambda d: to_peer(
            far_slots, "tile", my_tile, tiles, far_sems.at[stage], d).wait_send())


def on_device(tiles, passes, obs_local, obs_value, obs_weight, seg_tiles, comp_scale, comp_orient, comp_place):
    seg_count, fan_out = seg_tiles.shape
    points = obs_value.shape[0]
    seg_length = points // seg_count
    vmem = pl.BlockSpec(memory_space=pltpu.VMEM)
    coefficients, field = pl.pallas_call(
        functools.partial(kernel, tiles, passes),
        out_shape=(
            jax.ShapeDtypeStruct((1, LANES), jnp.float32),
            jax.ShapeDtypeStruct((8, LANES), jnp.float32),
        ),
        in_specs=[vmem, vmem, vmem, pl.BlockSpec(memory_space=pltpu.SMEM), vmem, vmem, vmem],
        out_specs=(vmem, vmem),
        scratch_shapes=[
            pltpu.VMEM((tiles, 8, LANES), jnp.float32),
            pltpu.VMEM((8, points), jnp.float32),
            pltpu.VMEM((points, 8), jnp.float32),
            pltpu.VMEM((seg_count * fan_out, seg_length, LANES), jnp.float32),
            pltpu.VMEM((2, tiles, LANES), jnp.float32),
            pltpu.VMEM((3, GX, 2 * LANES), jnp.float32),
            pltpu.VMEM((3, LANES, 2 * LANES), jnp.float32),
            pltpu.VMEM((2, passes, tiles, LANES), jnp.float32),
            pltpu.VMEM((2, tiles, tiles, LANES), jnp.float32),
            pltpu.VMEM((passes, 1, LANES), jnp.float32),
            pltpu.VMEM((tiles, 1, LANES), jnp.float32),
            pltpu.SemaphoreType.DMA((2, tiles)),
            pltpu.SemaphoreType.DMA((3, 2, passes)),
            pltpu.SemaphoreType.DMA((3, 2, tiles)),
        ],
        compiler_params=pltpu.CompilerParams(
            collective_id=0, has_side_effects=True, vmem_limit_bytes=40 * 2**20
        ),
    )(
        obs_local,
        obs_value.reshape(1, points),
        obs_weight.reshape(1, points),
        seg_tiles,
        comp_scale.reshape(1, -1),
        comp_orient.reshape(1, -1),
        comp_place.reshape(1, -1),
    )
    return coefficients.reshape(-1), field.reshape(1, 1, GX * GY)


def solution(mesh):
    return jax.shard_map(
        functools.partial(on_device, mesh.shape["tile"], mesh.shape["pass"]),
        mesh=mesh,
        in_specs=(
            P(None, None, ("tile", "pass")),
            P(("tile", "pass")),
            P(("tile", "pass")),
            P(("tile", "pass"), None),
            P("tile"),
            P("tile"),
            P("tile"),
        ),
        out_specs=(P("tile"), P("tile", "pass", None)),
        check_vma=False,
    )
```

```python
import functools
import math

import jax
import jax.numpy as jnp
import numpy as np
from jax import lax
from jax.experimental import pallas as pl
from jax.experimental.pallas import tpu as pltpu
from jax.sharding import PartitionSpec as P

GX = 32
GY = 32
LANES = 128
TIME_RATE = 8.0
LOG2E = math.log2(math.e)
TIME_SCALE = math.sqrt(TIME_RATE * LOG2E)
HIGHEST = lax.Precision.HIGHEST
MESH = pl.DeviceIdType.MESH


def cosine_polynomial(degree):
    fit = np.polynomial.Chebyshev.interpolate(
        lambda z: np.cos(2 * np.pi * np.sqrt(np.maximum(z, 0.0))), degree, domain=[0.0, 0.25]
    )
    return [float(c) for c in fit.convert(kind=np.polynomial.Polynomial).coef]


COSINE = cosine_polynomial(6)


def cos_turns(turns):
    part = turns - jnp.round(turns)
    square = part * part
    total = jnp.full_like(square, COSINE[-1])
    for coefficient in COSINE[-2::-1]:
        total = total * square + coefficient
    return total


def peers(count, body):
    if count <= 8:
        for distance in range(1, count):
            body(distance)
    else:

        def step(distance, carry):
            body(distance)
            return carry

        lax.fori_loop(1, count, step, 0)


def total_of(value):
    return jnp.sum(jnp.sum(value, axis=1, keepdims=True), axis=0, keepdims=True)


def kernel(
    tiles, passes, obs_in, value_in, weight_in, seg_in, scale_in, orient_in, place_in,
    coef_ref, field_ref,
    obs_ref, value_ref, weight_ref, seg_ref, scale_ref, orient_ref, place_ref, input_sems,
    table, stack, wide, basis, vectors, grid_x, grid_y,
    near, far, last, table_sems, near_sems, far_sems, last_sems,
):
    my_tile, my_pass = lax.axis_index("tile"), lax.axis_index("pass")
    fan_out, seg_count = seg_ref.shape
    points = value_ref.shape[1]
    seg_length = points // seg_count

    inputs = [
        pltpu.make_async_copy(source, target, input_sems.at[place])
        for place, (source, target) in enumerate((
            (scale_in, scale_ref), (orient_in, orient_ref), (place_in, place_ref),
            (obs_in, obs_ref), (value_in, value_ref), (weight_in, weight_ref), (seg_in, seg_ref),
        ))
    ]
    for copy in inputs:
        copy.start()

    barrier = pltpu.get_barrier_semaphore()
    peers(passes, lambda d: pl.semaphore_signal(
        barrier, inc=1, device_id={"pass": lax.rem(my_pass + d, passes)}, device_id_type=MESH))
    peers(tiles, lambda d: pl.semaphore_signal(
        barrier, inc=1, device_id={"tile": lax.rem(my_tile + d, tiles)}, device_id_type=MESH))

    def to_peer(buffer, axis, me, count, sems, distance):
        return pltpu.make_async_remote_copy(
            src_ref=buffer.at[me],
            dst_ref=buffer.at[me],
            send_sem=sems.at[0, distance],
            recv_sem=sems.at[1, distance],
            device_id={axis: lax.rem(me + distance, count)},
            device_id_type=MESH,
        )

    for copy in inputs[:3]:
        copy.wait()
    level = scale_ref[...].astype(jnp.float32)
    width = 0.4 * jnp.exp(level * math.log(0.7))
    wave = 2.2 / (2.0 * math.pi) / width
    turns = orient_ref[...].astype(jnp.float32) / 16.0
    place = place_ref[...]
    table[my_tile, 0:1, :] = ((place & 7).astype(jnp.float32) + 0.5) / 8.0
    table[my_tile, 1:2, :] = (((place >> 3) & 7).astype(jnp.float32) + 0.5) / 8.0
    table[my_tile, 2:3, :] = ((place >> 6).astype(jnp.float32) + 0.5) * (TIME_SCALE / 8.0)
    table[my_tile, 3:4, :] = 0.5 * LOG2E / (width * width)
    table[my_tile, 4:5, :] = wave * cos_turns(turns)
    table[my_tile, 5:6, :] = wave * cos_turns(turns - 0.25)
    table[my_tile, 6:7, :] = 2.0 * jnp.exp(level * math.log(1.5))
    table[my_tile, 7:8, :] = jnp.zeros((1, LANES), jnp.float32)

    pl.semaphore_wait(barrier, passes + tiles - 2)
    peers(tiles, lambda d: to_peer(table, "tile", my_tile, tiles, table_sems, d).start())

    for copy in inputs[3:]:
        copy.wait()
    roots = jnp.sqrt(weight_ref[...])
    for route in range(fan_out):
        for axis in range(3):
            line = obs_ref[axis, route : route + 1, :]
            row = 3 * route + axis
            stack[row : row + 1, :] = line * TIME_SCALE if axis == 2 else line
    root_row, value_row = 3 * fan_out, 3 * fan_out + 1
    stack[root_row : root_row + 1, :] = roots
    stack[value_row : value_row + 1, :] = roots * value_ref[...]

    def widen(block, carry):
        start = pl.multiple_of(block * LANES, LANES)
        columns = stack[:, pl.ds(start, LANES)].T
        for which in range(value_row + 1):
            wide[which, pl.ds(start, LANES), :] = jnp.broadcast_to(
                columns[:, which : which + 1], (LANES, LANES)
            )
        return carry

    lax.fori_loop(0, points // LANES, widen, 0)

    def column(seg, which):
        return wide[which, pl.ds(pl.multiple_of(seg * seg_length, seg_length), seg_length), :]

    peers(tiles, lambda d: to_peer(table, "tile", my_tile, tiles, table_sems, d).wait_recv())

    tile_row = lax.broadcasted_iota(jnp.int32, (tiles, LANES), 0)

    def gather_into(running, tile, block):
        part = jnp.sum(block, axis=0, keepdims=True)
        return running + jnp.where(tile_row == tile, part, 0.0)

    def build(seg, running):
        root, weighted = column(seg, root_row), column(seg, value_row)
        for route in range(fan_out):
            tile = seg_ref[route, seg]
            param = lambda row: table[tile, row : row + 1, :]
            delta_x = column(seg, 3 * route) - param(0)
            delta_y = column(seg, 3 * route + 1) - param(1)
            delta_t = column(seg, 3 * route + 2) - param(2)
            envelope = jnp.exp2(
                -(delta_x * delta_x + delta_y * delta_y) * param(3) - delta_t * delta_t
            )
            phi = envelope * root * cos_turns(delta_x * param(4) + delta_y * param(5))
            basis[seg * fan_out + route] = phi
            running = gather_into(running, tile, phi * weighted)
        return running

    def forward(which, seg):
        total = jnp.zeros((seg_length, LANES), jnp.float32)
        for route in range(fan_out):
            tile = seg_ref[route, seg]
            total = total + basis[seg * fan_out + route] * vectors[which, pl.ds(tile, 1), :]
        return jnp.sum(total, axis=1, keepdims=True)

    def normal(seg, running):
        weighted = forward(0, seg)
        for route in range(fan_out):
            running = gather_into(
                running, seg_ref[route, seg], basis[seg * fan_out + route] * weighted
            )
        return running

    def energy(seg, running):
        values = forward(1, seg)
        return running + values * values

    def sum_slots(buffer, count):
        if count <= 8:
            total = buffer[0]
            for slot in range(1, count):
                total = total + buffer[slot]
            return total
        return lax.fori_loop(1, count, lambda slot, total: total + buffer[slot], buffer[0])

    def all_sum(value, near_slots, far_slots, near_sem, far_sem, beside=None):
        near_slots[my_pass] = value
        peers(passes, lambda d: to_peer(near_slots, "pass", my_pass, passes, near_sem, d).start())
        if beside is not None:
            beside[0]()
        peers(passes, lambda d: to_peer(near_slots, "pass", my_pass, passes, near_sem, d).wait_recv())
        far_slots[my_tile] = sum_slots(near_slots, passes)
        peers(tiles, lambda d: to_peer(far_slots, "tile", my_tile, tiles, far_sem, d).start())
        if beside is not None:
            beside[1]()
        peers(tiles, lambda d: to_peer(far_slots, "tile", my_tile, tiles, far_sem, d).wait_recv())
        return sum_slots(far_slots, tiles)

    def grid_params(neighbor):
        tile = lax.rem(my_tile + (neighbor - 1) + tiles, tiles)
        return tile, lambda row: table[tile, row : row + 1, :]

    def axis_factors(delta, inverse, wave_row):
        envelope = jnp.exp2(-(delta * delta) * inverse)
        phase = delta * wave_row
        return envelope * cos_turns(phase), envelope * cos_turns(phase - 0.25)

    def grid_factors_y():
        cell = lax.broadcasted_iota(jnp.int32, (LANES, LANES), 0) & (GY - 1)
        place_y = (cell.astype(jnp.float32) + 0.5) / GY
        for neighbor in range(3):
            _, param = grid_params(neighbor)
            even, odd = axis_factors(place_y - param(1), param(3), param(5))
            grid_y[neighbor, :, :LANES] = even
            grid_y[neighbor, :, LANES:] = odd

    def grid_factors_x():
        row = lax.broadcasted_iota(jnp.int32, (GX, LANES), 0)
        cell = (row & 7) * (GX // 8) + (row >> 3)
        place_x = (cell.astype(jnp.float32) + 0.5) / GX
        day = (my_pass.astype(jnp.float32) + 0.5) / passes * TIME_SCALE
        for neighbor in range(3):
            _, param = grid_params(neighbor)
            even, odd = axis_factors(
                place_x - (param(0) + float(neighbor - 1)), param(3), param(4)
            )
            delta_t = day - param(2)
            in_time = jnp.exp2(-(delta_t * delta_t))
            grid_x[neighbor, :, :LANES] = even * in_time
            grid_x[neighbor, :, LANES:] = -odd * in_time

    zeros = jnp.zeros((tiles, LANES), jnp.float32)
    rhs = all_sum(
        lax.fori_loop(0, seg_count, build, zeros, unroll=2),
        near.at[0], far.at[0], near_sems.at[0], far_sems.at[0],
        (grid_factors_x, grid_factors_y),
    )
    norm_first = total_of(rhs * rhs)
    prior = table[:, 6, :]
    vectors[0] = rhs
    image = all_sum(
        lax.fori_loop(0, seg_count, normal, zeros, unroll=8),
        near.at[1], far.at[1], near_sems.at[1], far_sems.at[1],
    ) + prior * rhs
    step_first = norm_first / total_of(rhs * image)
    residual = rhs - step_first * image
    norm_next = total_of(residual * residual)
    direction = residual + norm_next / norm_first * rhs
    vectors[1] = direction

    fields = []

    def grid_fields():
        total = None
        for neighbor in range(3):
            tile, _ = grid_params(neighbor)
            parts = []
            for which in range(2):
                row = vectors[which, pl.ds(tile, 1), :]
                parts.append(grid_x[neighbor] * jnp.concatenate([row, row], axis=1))
            term = lax.dot_general(
                jnp.concatenate(parts, axis=0),
                grid_y[neighbor],
                (((1,), (1,)), ((), ())),
                precision=HIGHEST,
                preferred_element_type=jnp.float32,
            )
            total = term if total is None else total + term
        group = lax.broadcasted_iota(jnp.int32, (8, LANES), 1) // GY
        for begin in (0, GX):
            field = jnp.zeros((8, LANES), jnp.float32)
            for part in range(GX // 8):
                field = field + jnp.where(
                    group == part, total[begin + 8 * part : begin + 8 * part + 8, :], 0.0
                )
            fields.append(field)

    energies = lax.fori_loop(
        0, seg_count, energy, jnp.zeros((seg_length, 1), jnp.float32), unroll=8
    )
    me, everyone = my_tile * passes + my_pass, tiles * passes

    def to_anyone(distance):
        other = lax.rem(me + distance, everyone)
        return pltpu.make_async_remote_copy(
            src_ref=last.at[me],
            dst_ref=last.at[me],
            send_sem=last_sems.at[0, distance],
            recv_sem=last_sems.at[1, distance],
            device_id={"tile": other // passes, "pass": lax.rem(other, passes)},
            device_id_type=MESH,
        )

    last[me] = jnp.broadcast_to(jnp.sum(energies, axis=0, keepdims=True), (1, LANES))
    peers(everyone, lambda d: to_anyone(d).start())
    grid_fields()
    prior_product = total_of(direction * direction * prior)
    peers(everyone, lambda d: to_anyone(d).wait_recv())
    product = jnp.sum(last[:, 0, :], axis=0, keepdims=True)[:, 0:1] + prior_product
    step_second = norm_next / product
    mine = pl.ds(my_tile, 1)
    coef_ref[...] = step_first * vectors[0, mine, :] + step_second * vectors[1, mine, :]
    field_ref[...] = step_first * fields[0] + step_second * fields[1]

    peers(tiles, lambda d: to_peer(table, "tile", my_tile, tiles, table_sems, d).wait_send())
    for stage in range(2):
        peers(passes, lambda d: to_peer(
            near.at[stage], "pass", my_pass, passes, near_sems.at[stage], d).wait_send())
        peers(tiles, lambda d: to_peer(
            far.at[stage], "tile", my_tile, tiles, far_sems.at[stage], d).wait_send())
    peers(everyone, lambda d: to_anyone(d).wait_send())


def on_device(tiles, passes, obs_local, obs_value, obs_weight, seg_tiles, comp_scale, comp_orient, comp_place):
    seg_count, fan_out = seg_tiles.shape
    points = obs_value.shape[0]
    seg_length = points // seg_count
    vmem = pl.BlockSpec(memory_space=pltpu.VMEM)
    coefficients, field = pl.pallas_call(
        functools.partial(kernel, tiles, passes),
        out_shape=(
            jax.ShapeDtypeStruct((1, LANES), jnp.float32),
            jax.ShapeDtypeStruct((8, LANES), jnp.float32),
        ),
        in_specs=[pl.BlockSpec(memory_space=pl.ANY)] * 7,
        out_specs=(vmem, vmem),
        scratch_shapes=[
            pltpu.VMEM((3, fan_out, points), jnp.float32),
            pltpu.VMEM((1, points), jnp.float32),
            pltpu.VMEM((1, points), jnp.float32),
            pltpu.SMEM((fan_out, seg_count), jnp.int32),
            pltpu.VMEM((1, LANES), jnp.int32),
            pltpu.VMEM((1, LANES), jnp.int32),
            pltpu.VMEM((1, LANES), jnp.int32),
            pltpu.SemaphoreType.DMA((7,)),
            pltpu.VMEM((tiles, 8, LANES), jnp.float32),
            pltpu.VMEM((3 * fan_out + 2, points), jnp.float32),
            pltpu.VMEM((3 * fan_out + 2, points, LANES), jnp.float32),
            pltpu.VMEM((seg_count * fan_out, seg_length, LANES), jnp.float32),
            pltpu.VMEM((2, tiles, LANES), jnp.float32),
            pltpu.VMEM((3, GX, 2 * LANES), jnp.float32),
            pltpu.VMEM((3, LANES, 2 * LANES), jnp.float32),
            pltpu.VMEM((2, passes, tiles, LANES), jnp.float32),
            pltpu.VMEM((2, tiles, tiles, LANES), jnp.float32),
            pltpu.VMEM((tiles * passes, 1, LANES), jnp.float32),
            pltpu.SemaphoreType.DMA((2, tiles)),
            pltpu.SemaphoreType.DMA((2, 2, passes)),
            pltpu.SemaphoreType.DMA((2, 2, tiles)),
            pltpu.SemaphoreType.DMA((2, tiles * passes)),
        ],
        compiler_params=pltpu.CompilerParams(
            collective_id=0, has_side_effects=True, vmem_limit_bytes=60 * 2**20
        ),
    )(
        obs_local.transpose(1, 0, 2),
        obs_value.reshape(1, points),
        obs_weight.reshape(1, points),
        seg_tiles.T,
        comp_scale.reshape(1, -1),
        comp_orient.reshape(1, -1),
        comp_place.reshape(1, -1),
    )
    return coefficients.reshape(-1), field.reshape(1, 1, GX * GY)


def solution(mesh):
    return jax.shard_map(
        functools.partial(on_device, mesh.shape["tile"], mesh.shape["pass"]),
        mesh=mesh,
        in_specs=(
            P(None, None, ("tile", "pass")),
            P(("tile", "pass")),
            P(("tile", "pass")),
            P(("tile", "pass"), None),
            P("tile"),
            P("tile"),
            P("tile"),
        ),
        out_specs=(P("tile"), P("tile", "pass", None)),
        check_vma=False,
    )
```

```python
import functools
import math

import jax
import jax.numpy as jnp
import numpy as np
from jax import lax
from jax.experimental import pallas as pl
from jax.experimental.pallas import tpu as pltpu
from jax.sharding import PartitionSpec as P

GX = 32
GY = 32
LANES = 128
TIME_RATE = 8.0
LOG2E = math.log2(math.e)
TIME_SCALE = math.sqrt(TIME_RATE * LOG2E)
HIGHEST = lax.Precision.HIGHEST
MESH = pl.DeviceIdType.MESH


def cosine_polynomial(degree):
    fit = np.polynomial.Chebyshev.interpolate(
        lambda z: np.cos(2 * np.pi * np.sqrt(np.maximum(z, 0.0))), degree, domain=[0.0, 0.25]
    )
    return [float(c) for c in fit.convert(kind=np.polynomial.Polynomial).coef]


COSINE = cosine_polynomial(6)


def cos_turns(turns):
    part = turns - jnp.round(turns)
    square = part * part
    total = jnp.full_like(square, COSINE[-1])
    for coefficient in COSINE[-2::-1]:
        total = total * square + coefficient
    return total


def peers(count, body):
    if count <= 32:
        for distance in range(1, count):
            body(distance)
    else:

        def step(distance, carry):
            body(distance)
            return carry

        lax.fori_loop(1, count, step, 0)


def total_of(value):
    return jnp.sum(jnp.sum(value, axis=1, keepdims=True), axis=0, keepdims=True)


def kernel(
    tiles, passes, obs_in, value_in, weight_in, seg_in, scale_in, orient_in, place_in,
    coef_ref, field_ref,
    obs_ref, value_ref, weight_ref, seg_ref, scale_ref, orient_ref, place_ref, input_sems,
    table, stack, wide, basis, vectors, grid_x, grid_y,
    near, far, last, table_sems, near_sems, far_sems, last_sems,
):
    my_tile, my_pass = lax.axis_index("tile"), lax.axis_index("pass")
    fan_out, seg_count = seg_ref.shape
    points = value_ref.shape[1]
    seg_length = points // seg_count

    inputs = [
        pltpu.make_async_copy(source, target, input_sems.at[place])
        for place, (source, target) in enumerate((
            (scale_in, scale_ref), (orient_in, orient_ref), (place_in, place_ref),
            (obs_in, obs_ref), (value_in, value_ref), (weight_in, weight_ref), (seg_in, seg_ref),
        ))
    ]
    for copy in inputs:
        copy.start()

    barrier = pltpu.get_barrier_semaphore()
    peers(passes, lambda d: pl.semaphore_signal(
        barrier, inc=1, device_id={"pass": lax.rem(my_pass + d, passes)}, device_id_type=MESH))
    peers(tiles, lambda d: pl.semaphore_signal(
        barrier, inc=1, device_id={"tile": lax.rem(my_tile + d, tiles)}, device_id_type=MESH))

    def to_peer(buffer, axis, me, count, sems, distance):
        return pltpu.make_async_remote_copy(
            src_ref=buffer.at[me],
            dst_ref=buffer.at[me],
            send_sem=sems.at[0],
            recv_sem=sems.at[1],
            device_id={axis: lax.rem(me + distance, count)},
            device_id_type=MESH,
        )

    for copy in inputs[:3]:
        copy.wait()
    def wait_for_peers(buffer, count, sem):
        slots = buffer.at[pl.ds(0, count - 1)]
        pltpu.make_async_copy(slots, slots, sem).wait()

    level = scale_ref[...].astype(jnp.float32)
    width = 0.4 * jnp.exp(level * math.log(0.7))
    wave = 2.2 / (2.0 * math.pi) / width
    turns = orient_ref[...].astype(jnp.float32) / 16.0
    place = place_ref[...]
    table[my_tile, 0:1, :] = ((place & 7).astype(jnp.float32) + 0.5) / 8.0
    table[my_tile, 1:2, :] = (((place >> 3) & 7).astype(jnp.float32) + 0.5) / 8.0
    table[my_tile, 2:3, :] = ((place >> 6).astype(jnp.float32) + 0.5) * (TIME_SCALE / 8.0)
    table[my_tile, 3:4, :] = 0.5 * LOG2E / (width * width)
    table[my_tile, 4:5, :] = wave * cos_turns(turns)
    table[my_tile, 5:6, :] = wave * cos_turns(turns - 0.25)
    table[my_tile, 6:7, :] = 2.0 * jnp.exp(level * math.log(1.5))
    table[my_tile, 7:8, :] = jnp.zeros((1, LANES), jnp.float32)

    pl.semaphore_wait(barrier, passes + tiles - 2)
    peers(tiles, lambda d: to_peer(table, "tile", my_tile, tiles, table_sems, d).start())

    for copy in inputs[3:]:
        copy.wait()
    roots = jnp.sqrt(weight_ref[...])
    for route in range(fan_out):
        for axis in range(3):
            line = obs_ref[axis, route : route + 1, :]
            row = 3 * route + axis
            stack[row : row + 1, :] = line * TIME_SCALE if axis == 2 else line
    root_row, value_row = 3 * fan_out, 3 * fan_out + 1
    stack[root_row : root_row + 1, :] = roots
    stack[value_row : value_row + 1, :] = roots * value_ref[...]

    def widen(block, carry):
        start = pl.multiple_of(block * LANES, LANES)
        columns = stack[:, pl.ds(start, LANES)].T
        for which in range(value_row + 1):
            wide[which, pl.ds(start, LANES), :] = jnp.broadcast_to(
                columns[:, which : which + 1], (LANES, LANES)
            )
        return carry

    lax.fori_loop(0, points // LANES, widen, 0, unroll=4)

    def column(seg, which):
        return wide[which, pl.ds(pl.multiple_of(seg * seg_length, seg_length), seg_length), :]

    wait_for_peers(table, tiles, table_sems.at[1])

    tile_row = lax.broadcasted_iota(jnp.int32, (tiles, LANES), 0)

    def gather_into(running, tile, block):
        part = jnp.sum(block, axis=0, keepdims=True)
        return running + jnp.where(tile_row == tile, part, 0.0)

    def build(seg, running):
        root, weighted = column(seg, root_row), column(seg, value_row)
        for route in range(fan_out):
            tile = seg_ref[route, seg]
            param = lambda row: table[tile, row : row + 1, :]
            delta_x = column(seg, 3 * route) - param(0)
            delta_y = column(seg, 3 * route + 1) - param(1)
            delta_t = column(seg, 3 * route + 2) - param(2)
            envelope = jnp.exp2(
                -(delta_x * delta_x + delta_y * delta_y) * param(3) - delta_t * delta_t
            )
            phi = envelope * root * cos_turns(delta_x * param(4) + delta_y * param(5))
            basis[seg * fan_out + route] = phi
            running = gather_into(running, tile, phi * weighted)
        return running

    def forward(which, seg):
        total = jnp.zeros((seg_length, LANES), jnp.float32)
        for route in range(fan_out):
            tile = seg_ref[route, seg]
            total = total + basis[seg * fan_out + route] * vectors[which, pl.ds(tile, 1), :]
        return jnp.sum(total, axis=1, keepdims=True)

    def normal(seg, running):
        weighted = forward(0, seg)
        for route in range(fan_out):
            running = gather_into(
                running, seg_ref[route, seg], basis[seg * fan_out + route] * weighted
            )
        return running

    def energy(seg, running):
        values = forward(1, seg)
        return running + values * values

    def sum_slots(buffer, count):
        if count <= 8:
            total = buffer[0]
            for slot in range(1, count):
                total = total + buffer[slot]
            return total
        return lax.fori_loop(1, count, lambda slot, total: total + buffer[slot], buffer[0])

    def all_sum(value, near_slots, far_slots, near_sem, far_sem, beside=None):
        near_slots[my_pass] = value
        peers(passes, lambda d: to_peer(near_slots, "pass", my_pass, passes, near_sem, d).start())
        if beside is not None:
            beside[0]()
        wait_for_peers(near_slots, passes, near_sem.at[1])
        far_slots[my_tile] = sum_slots(near_slots, passes)
        peers(tiles, lambda d: to_peer(far_slots, "tile", my_tile, tiles, far_sem, d).start())
        if beside is not None:
            beside[1]()
        wait_for_peers(far_slots, tiles, far_sem.at[1])
        return sum_slots(far_slots, tiles)

    def grid_params(neighbor):
        tile = lax.rem(my_tile + (neighbor - 1) + tiles, tiles)
        return tile, lambda row: table[tile, row : row + 1, :]

    def axis_factors(delta, inverse, wave_row):
        envelope = jnp.exp2(-(delta * delta) * inverse)
        phase = delta * wave_row
        return envelope * cos_turns(phase), envelope * cos_turns(phase - 0.25)

    def grid_factors_y():
        cell = lax.broadcasted_iota(jnp.int32, (LANES, LANES), 0) & (GY - 1)
        place_y = (cell.astype(jnp.float32) + 0.5) / GY
        for neighbor in range(3):
            _, param = grid_params(neighbor)
            even, odd = axis_factors(place_y - param(1), param(3), param(5))
            grid_y[neighbor, :, :LANES] = even
            grid_y[neighbor, :, LANES:] = odd

    def grid_factors_x():
        row = lax.broadcasted_iota(jnp.int32, (GX, LANES), 0)
        cell = (row & 7) * (GX // 8) + (row >> 3)
        place_x = (cell.astype(jnp.float32) + 0.5) / GX
        day = (my_pass.astype(jnp.float32) + 0.5) / passes * TIME_SCALE
        for neighbor in range(3):
            _, param = grid_params(neighbor)
            even, odd = axis_factors(
                place_x - (param(0) + float(neighbor - 1)), param(3), param(4)
            )
            delta_t = day - param(2)
            in_time = jnp.exp2(-(delta_t * delta_t))
            grid_x[neighbor, :, :LANES] = even * in_time
            grid_x[neighbor, :, LANES:] = -odd * in_time

    zeros = jnp.zeros((tiles, LANES), jnp.float32)
    rhs = all_sum(
        lax.fori_loop(0, seg_count, build, zeros, unroll=4),
        near.at[0], far.at[0], near_sems.at[0], far_sems.at[0],
        (grid_factors_x, grid_factors_y),
    )
    prior, norms = table[:, 6, :], []
    vectors[0] = rhs
    image = all_sum(
        lax.fori_loop(0, seg_count, normal, zeros, unroll=8),
        near.at[1], far.at[1], near_sems.at[1], far_sems.at[1],
        (lambda: norms.append(total_of(rhs * rhs)), lambda: None),
    ) + prior * rhs
    norm_first = norms[0]
    step_first = norm_first / total_of(rhs * image)
    residual = rhs - step_first * image
    norm_next = total_of(residual * residual)
    direction = residual + norm_next / norm_first * rhs
    vectors[1] = direction

    fields = []

    def grid_fields():
        total = None
        for neighbor in range(3):
            tile, _ = grid_params(neighbor)
            parts = []
            for which in range(2):
                row = vectors[which, pl.ds(tile, 1), :]
                parts.append(grid_x[neighbor] * jnp.concatenate([row, row], axis=1))
            term = lax.dot_general(
                jnp.concatenate(parts, axis=0),
                grid_y[neighbor],
                (((1,), (1,)), ((), ())),
                precision=HIGHEST,
                preferred_element_type=jnp.float32,
            )
            total = term if total is None else total + term
        group = lax.broadcasted_iota(jnp.int32, (8, LANES), 1) // GY
        for begin in (0, GX):
            field = jnp.zeros((8, LANES), jnp.float32)
            for part in range(GX // 8):
                field = field + jnp.where(
                    group == part, total[begin + 8 * part : begin + 8 * part + 8, :], 0.0
                )
            fields.append(field)

    energies = lax.fori_loop(
        0, seg_count, energy, jnp.zeros((seg_length, 1), jnp.float32), unroll=8
    )
    me, everyone = my_tile * passes + my_pass, tiles * passes

    def to_anyone(distance):
        other = lax.rem(me + distance, everyone)
        return pltpu.make_async_remote_copy(
            src_ref=last.at[me],
            dst_ref=last.at[me],
            send_sem=last_sems.at[0],
            recv_sem=last_sems.at[1],
            device_id={"tile": other // passes, "pass": lax.rem(other, passes)},
            device_id_type=MESH,
        )

    last[me] = jnp.broadcast_to(jnp.sum(energies, axis=0, keepdims=True), (1, LANES))
    peers(everyone, lambda d: to_anyone(d).start())
    grid_fields()
    prior_product = total_of(direction * direction * prior)
    wait_for_peers(last, everyone, last_sems.at[1])
    product = jnp.sum(last[:, 0, :], axis=0, keepdims=True)[:, 0:1] + prior_product
    step_second = norm_next / product
    mine = pl.ds(my_tile, 1)
    coef_ref[...] = step_first * vectors[0, mine, :] + step_second * vectors[1, mine, :]
    field_ref[...] = step_first * fields[0] + step_second * fields[1]

    wait_for_peers(table, tiles, table_sems.at[0])
    for stage in range(2):
        wait_for_peers(near.at[stage], passes, near_sems.at[stage, 0])
        wait_for_peers(far.at[stage], tiles, far_sems.at[stage, 0])
    wait_for_peers(last, everyone, last_sems.at[0])


def hand_over(coef_in, field_in, coef_ref, field_ref, sems):
    copies = [
        pltpu.make_async_copy(coef_in, coef_ref, sems.at[0]),
        pltpu.make_async_copy(field_in, field_ref, sems.at[1]),
    ]
    for copy in copies:
        copy.start()
    for copy in copies:
        copy.wait()


def on_device(tiles, passes, obs_local, obs_value, obs_weight, seg_tiles, comp_scale, comp_orient, comp_place):
    seg_count, fan_out = seg_tiles.shape
    points = obs_value.shape[0]
    seg_length = points // seg_count
    vmem = pl.BlockSpec(memory_space=pltpu.VMEM)
    coefficients, field = pl.pallas_call(
        functools.partial(kernel, tiles, passes),
        out_shape=(
            jax.ShapeDtypeStruct((1, LANES), jnp.float32),
            jax.ShapeDtypeStruct((8, LANES), jnp.float32),
        ),
        in_specs=[pl.BlockSpec(memory_space=pl.ANY)] * 7,
        out_specs=(vmem, vmem),
        scratch_shapes=[
            pltpu.VMEM((3, fan_out, points), jnp.float32),
            pltpu.VMEM((1, points), jnp.float32),
            pltpu.VMEM((1, points), jnp.float32),
            pltpu.SMEM((fan_out, seg_count), jnp.int32),
            pltpu.VMEM((1, LANES), jnp.int32),
            pltpu.VMEM((1, LANES), jnp.int32),
            pltpu.VMEM((1, LANES), jnp.int32),
            pltpu.SemaphoreType.DMA((7,)),
            pltpu.VMEM((tiles, 8, LANES), jnp.float32),
            pltpu.VMEM((3 * fan_out + 2, points), jnp.float32),
            pltpu.VMEM((3 * fan_out + 2, points, LANES), jnp.float32),
            pltpu.VMEM((seg_count * fan_out, seg_length, LANES), jnp.float32),
            pltpu.VMEM((2, tiles, LANES), jnp.float32),
            pltpu.VMEM((3, GX, 2 * LANES), jnp.float32),
            pltpu.VMEM((3, LANES, 2 * LANES), jnp.float32),
            pltpu.VMEM((2, passes, tiles, LANES), jnp.float32),
            pltpu.VMEM((2, tiles, tiles, LANES), jnp.float32),
            pltpu.VMEM((tiles * passes, 1, LANES), jnp.float32),
            pltpu.SemaphoreType.DMA((2,)),
            pltpu.SemaphoreType.DMA((2, 2)),
            pltpu.SemaphoreType.DMA((2, 2)),
            pltpu.SemaphoreType.DMA((2,)),
        ],
        compiler_params=pltpu.CompilerParams(
            collective_id=0, has_side_effects=True, vmem_limit_bytes=60 * 2**20
        ),
    )(
        obs_local.transpose(1, 0, 2),
        obs_value.reshape(1, points),
        obs_weight.reshape(1, points),
        seg_tiles.T,
        comp_scale.reshape(1, -1),
        comp_orient.reshape(1, -1),
        comp_place.reshape(1, -1),
    )
    anywhere = pl.BlockSpec(memory_space=pl.ANY)
    coefficients, field = pl.pallas_call(
        hand_over,
        out_shape=(
            jax.ShapeDtypeStruct((1, LANES), jnp.float32),
            jax.ShapeDtypeStruct((8, LANES), jnp.float32),
        ),
        in_specs=[anywhere, anywhere],
        out_specs=(anywhere, anywhere),
        scratch_shapes=[pltpu.SemaphoreType.DMA((2,))],
        compiler_params=pltpu.CompilerParams(vmem_limit_bytes=60 * 2**20),
    )(coefficients, field)
    return coefficients.reshape(-1), field.reshape(1, 1, GX * GY)


def solution(mesh):
    return jax.shard_map(
        functools.partial(on_device, mesh.shape["tile"], mesh.shape["pass"]),
        mesh=mesh,
        in_specs=(
            P(None, None, ("tile", "pass")),
            P(("tile", "pass")),
            P(("tile", "pass")),
            P(("tile", "pass"), None),
            P("tile"),
            P("tile"),
            P("tile"),
        ),
        out_specs=(P("tile"), P("tile", "pass", None)),
        check_vma=False,
    )
```

```python
import functools
import math

import jax
import jax.numpy as jnp
import numpy as np
from jax import lax
from jax.experimental import pallas as pl
from jax.experimental.pallas import tpu as pltpu
from jax.sharding import PartitionSpec as P

GX = 32
GY = 32
LANES = 128
TIME_RATE = 8.0
TIME_SCALE = math.sqrt(TIME_RATE)
HIGHEST = lax.Precision.HIGHEST
MESH = pl.DeviceIdType.MESH


def cosine_polynomial(degree):
    fit = np.polynomial.Chebyshev.interpolate(
        lambda z: np.cos(2 * np.pi * np.sqrt(np.maximum(z, 0.0))), degree, domain=[0.0, 0.25]
    )
    return [float(c) for c in fit.convert(kind=np.polynomial.Polynomial).coef]


COSINE = cosine_polynomial(6)


def cos_turns(turns):
    part = turns - jnp.round(turns)
    square = part * part
    total = jnp.full_like(square, COSINE[-1])
    for coefficient in COSINE[-2::-1]:
        total = total * square + coefficient
    return total


def peers(count, body):
    if count <= 32:
        for distance in range(1, count):
            body(distance)
    else:

        def step(distance, carry):
            body(distance)
            return carry

        lax.fori_loop(1, count, step, 0)


def total_of(value):
    return jnp.sum(jnp.sum(value, axis=1, keepdims=True), axis=0, keepdims=True)


def kernel(
    tiles, passes, obs_ref, value_ref, weight_ref, seg_ref, scale_ref, orient_ref, place_ref,
    coef_ref, field_ref,
    table, stack, wide, basis, vectors, grid_x, grid_y,
    near, far, last, table_sems, near_sems, far_sems, last_sems,
):
    my_tile, my_pass = lax.axis_index("tile"), lax.axis_index("pass")
    fan_out, seg_count = seg_ref.shape
    points = value_ref.shape[1]
    seg_length = points // seg_count

    barrier = pltpu.get_barrier_semaphore()
    peers(passes, lambda d: pl.semaphore_signal(
        barrier, inc=1, device_id={"pass": lax.rem(my_pass + d, passes)}, device_id_type=MESH))
    peers(tiles, lambda d: pl.semaphore_signal(
        barrier, inc=1, device_id={"tile": lax.rem(my_tile + d, tiles)}, device_id_type=MESH))

    def to_peer(buffer, axis, me, count, sems, distance):
        return pltpu.make_async_remote_copy(
            src_ref=buffer.at[me],
            dst_ref=buffer.at[me],
            send_sem=sems.at[0],
            recv_sem=sems.at[1],
            device_id={axis: lax.rem(me + distance, count)},
            device_id_type=MESH,
        )

    def wait_for_peers(buffer, count, sem):
        slots = buffer.at[pl.ds(0, count - 1)]
        pltpu.make_async_copy(slots, slots, sem).wait()

    level = scale_ref[...].astype(jnp.float32)
    width = 0.4 * jnp.exp(level * math.log(0.7))
    wave = 2.2 / (2.0 * math.pi) / width
    turns = orient_ref[...].astype(jnp.float32) / 16.0
    place = place_ref[...]
    table[my_tile, 0:1, :] = ((place & 7).astype(jnp.float32) + 0.5) / 8.0
    table[my_tile, 1:2, :] = (((place >> 3) & 7).astype(jnp.float32) + 0.5) / 8.0
    table[my_tile, 2:3, :] = ((place >> 6).astype(jnp.float32) + 0.5) * (TIME_SCALE / 8.0)
    table[my_tile, 3:4, :] = 0.5 / (width * width)
    table[my_tile, 4:5, :] = wave * cos_turns(turns)
    table[my_tile, 5:6, :] = wave * cos_turns(turns - 0.25)
    table[my_tile, 6:7, :] = 2.0 * jnp.exp(level * math.log(1.5))
    table[my_tile, 7:8, :] = jnp.zeros((1, LANES), jnp.float32)

    pl.semaphore_wait(barrier, passes + tiles - 2)
    peers(tiles, lambda d: to_peer(table, "tile", my_tile, tiles, table_sems, d).start())

    roots = jnp.sqrt(weight_ref[...])
    for route in range(fan_out):
        for axis in range(3):
            line = obs_ref[axis, route : route + 1, :]
            row = 3 * route + axis
            stack[row : row + 1, :] = line * TIME_SCALE if axis == 2 else line
    root_row, value_row = 3 * fan_out, 3 * fan_out + 1
    stack[root_row : root_row + 1, :] = roots
    stack[value_row : value_row + 1, :] = roots * value_ref[...]

    def widen(block, carry):
        start = pl.multiple_of(block * LANES, LANES)
        columns = stack[:, pl.ds(start, LANES)].T
        for which in range(value_row + 1):
            wide[which, pl.ds(start, LANES), :] = jnp.broadcast_to(
                columns[:, which : which + 1], (LANES, LANES)
            )
        return carry

    lax.fori_loop(0, points // LANES, widen, 0, unroll=4)

    def column(seg, which):
        return wide[which, pl.ds(pl.multiple_of(seg * seg_length, seg_length), seg_length), :]

    wait_for_peers(table, tiles, table_sems.at[1])

    tile_row = lax.broadcasted_iota(jnp.int32, (tiles, LANES), 0)

    def gather_into(running, tile, block):
        part = jnp.sum(block, axis=0, keepdims=True)
        return running + jnp.where(tile_row == tile, part, 0.0)

    def build(seg, running):
        root, weighted = column(seg, root_row), column(seg, value_row)
        for route in range(fan_out):
            tile = seg_ref[route, seg]
            param = lambda row: table[tile, row : row + 1, :]
            delta_x = column(seg, 3 * route) - param(0)
            delta_y = column(seg, 3 * route + 1) - param(1)
            delta_t = column(seg, 3 * route + 2) - param(2)
            envelope = jnp.exp(
                -(delta_x * delta_x + delta_y * delta_y) * param(3) - delta_t * delta_t
            )
            phi = envelope * root * cos_turns(delta_x * param(4) + delta_y * param(5))
            basis[seg * fan_out + route] = phi
            running = gather_into(running, tile, phi * weighted)
        return running

    def forward(which, seg):
        total = jnp.zeros((seg_length, LANES), jnp.float32)
        for route in range(fan_out):
            tile = seg_ref[route, seg]
            total = total + basis[seg * fan_out + route] * vectors[which, pl.ds(tile, 1), :]
        return jnp.sum(total, axis=1, keepdims=True)

    def normal(seg, running):
        weighted = forward(0, seg)
        for route in range(fan_out):
            running = gather_into(
                running, seg_ref[route, seg], basis[seg * fan_out + route] * weighted
            )
        return running

    def energy(seg, running):
        values = forward(1, seg)
        return running + values * values

    def sum_slots(buffer, count):
        if count <= 8:
            total = buffer[0]
            for slot in range(1, count):
                total = total + buffer[slot]
            return total
        return lax.fori_loop(1, count, lambda slot, total: total + buffer[slot], buffer[0])

    def all_sum(value, near_slots, far_slots, near_sem, far_sem, beside=None):
        near_slots[my_pass] = value
        peers(passes, lambda d: to_peer(near_slots, "pass", my_pass, passes, near_sem, d).start())
        if beside is not None:
            beside[0]()
        wait_for_peers(near_slots, passes, near_sem.at[1])
        far_slots[my_tile] = sum_slots(near_slots, passes)
        peers(tiles, lambda d: to_peer(far_slots, "tile", my_tile, tiles, far_sem, d).start())
        if beside is not None:
            beside[1]()
        wait_for_peers(far_slots, tiles, far_sem.at[1])
        return sum_slots(far_slots, tiles)

    def grid_params(neighbor):
        tile = lax.rem(my_tile + (neighbor - 1) + tiles, tiles)
        return tile, lambda row: table[tile, row : row + 1, :]

    def axis_factors(delta, inverse, wave_row):
        envelope = jnp.exp(-(delta * delta) * inverse)
        phase = delta * wave_row
        return envelope * cos_turns(phase), envelope * cos_turns(phase - 0.25)

    def grid_factors_y():
        cell = lax.broadcasted_iota(jnp.int32, (LANES, LANES), 0) & (GY - 1)
        place_y = (cell.astype(jnp.float32) + 0.5) / GY
        for neighbor in range(3):
            _, param = grid_params(neighbor)
            even, odd = axis_factors(place_y - param(1), param(3), param(5))
            grid_y[neighbor, :, :LANES] = even
            grid_y[neighbor, :, LANES:] = odd

    def grid_factors_x():
        row = lax.broadcasted_iota(jnp.int32, (GX, LANES), 0)
        cell = (row & 7) * (GX // 8) + (row >> 3)
        place_x = (cell.astype(jnp.float32) + 0.5) / GX
        day = (my_pass.astype(jnp.float32) + 0.5) / passes * TIME_SCALE
        for neighbor in range(3):
            _, param = grid_params(neighbor)
            even, odd = axis_factors(
                place_x - (param(0) + float(neighbor - 1)), param(3), param(4)
            )
            delta_t = day - param(2)
            in_time = jnp.exp(-(delta_t * delta_t))
            grid_x[neighbor, :, :LANES] = even * in_time
            grid_x[neighbor, :, LANES:] = -odd * in_time

    def grid_field(which):
        total = None
        for neighbor in range(3):
            tile, _ = grid_params(neighbor)
            row = vectors[which, pl.ds(tile, 1), :]
            term = lax.dot_general(
                grid_x[neighbor] * jnp.concatenate([row, row], axis=1),
                grid_y[neighbor],
                (((1,), (1,)), ((), ())),
                precision=HIGHEST,
                preferred_element_type=jnp.float32,
            )
            total = term if total is None else total + term
        group = lax.broadcasted_iota(jnp.int32, (8, LANES), 1) // GY
        field = jnp.zeros((8, LANES), jnp.float32)
        for part in range(GX // 8):
            field = field + jnp.where(group == part, total[8 * part : 8 * part + 8, :], 0.0)
        return field

    zeros = jnp.zeros((tiles, LANES), jnp.float32)
    rhs = all_sum(
        lax.fori_loop(0, seg_count, build, zeros, unroll=4),
        near.at[0], far.at[0], near_sems.at[0], far_sems.at[0],
        (grid_factors_x, grid_factors_y),
    )
    prior, norms, fields = table[:, 6, :], [], []
    vectors[0] = rhs
    image = all_sum(
        lax.fori_loop(0, seg_count, normal, zeros, unroll=8),
        near.at[1], far.at[1], near_sems.at[1], far_sems.at[1],
        (lambda: norms.append(total_of(rhs * rhs)), lambda: fields.append(grid_field(0))),
    ) + prior * rhs
    norm_first = norms[0]
    step_first = norm_first / total_of(rhs * image)
    residual = rhs - step_first * image
    norm_next = total_of(residual * residual)
    direction = residual + norm_next / norm_first * rhs
    vectors[1] = direction

    energies = lax.fori_loop(
        0, seg_count, energy, jnp.zeros((seg_length, 1), jnp.float32), unroll=8
    )
    me, everyone = my_tile * passes + my_pass, tiles * passes

    def to_anyone(distance):
        other = lax.rem(me + distance, everyone)
        return pltpu.make_async_remote_copy(
            src_ref=last.at[me],
            dst_ref=last.at[me],
            send_sem=last_sems.at[0],
            recv_sem=last_sems.at[1],
            device_id={"tile": other // passes, "pass": lax.rem(other, passes)},
            device_id_type=MESH,
        )

    last[me] = jnp.broadcast_to(jnp.sum(energies, axis=0, keepdims=True), (1, LANES))
    peers(everyone, lambda d: to_anyone(d).start())
    fields.append(grid_field(1))
    prior_product = total_of(direction * direction * prior)
    wait_for_peers(last, everyone, last_sems.at[1])
    product = jnp.sum(last[:, 0, :], axis=0, keepdims=True)[:, 0:1] + prior_product
    step_second = norm_next / product
    mine = pl.ds(my_tile, 1)
    coef_ref[...] = step_first * vectors[0, mine, :] + step_second * vectors[1, mine, :]
    field_ref[...] = step_first * fields[0] + step_second * fields[1]

    wait_for_peers(table, tiles, table_sems.at[0])
    for stage in range(2):
        wait_for_peers(near.at[stage], passes, near_sems.at[stage, 0])
        wait_for_peers(far.at[stage], tiles, far_sems.at[stage, 0])
    wait_for_peers(last, everyone, last_sems.at[0])


def hand_over(coef_in, field_in, coef_ref, field_ref, sems):
    copies = [
        pltpu.make_async_copy(coef_in, coef_ref, sems.at[0]),
        pltpu.make_async_copy(field_in, field_ref, sems.at[1]),
    ]
    for copy in copies:
        copy.start()
    for copy in copies:
        copy.wait()


def on_device(tiles, passes, obs_local, obs_value, obs_weight, seg_tiles, comp_scale, comp_orient, comp_place):
    seg_count, fan_out = seg_tiles.shape
    points = obs_value.shape[0]
    seg_length = points // seg_count
    vmem = pl.BlockSpec(memory_space=pltpu.VMEM)
    hbm = pl.BlockSpec(memory_space=pltpu.HBM)
    coefficients, field = pl.pallas_call(
        functools.partial(kernel, tiles, passes),
        out_shape=(
            jax.ShapeDtypeStruct((1, LANES), jnp.float32),
            jax.ShapeDtypeStruct((8, LANES), jnp.float32),
        ),
        in_specs=[vmem, vmem, vmem, pl.BlockSpec(memory_space=pltpu.SMEM), vmem, vmem, vmem],
        out_specs=(vmem, vmem),
        scratch_shapes=[
            pltpu.VMEM((tiles, 8, LANES), jnp.float32),
            pltpu.VMEM((3 * fan_out + 2, points), jnp.float32),
            pltpu.VMEM((3 * fan_out + 2, points, LANES), jnp.float32),
            pltpu.VMEM((seg_count * fan_out, seg_length, LANES), jnp.float32),
            pltpu.VMEM((2, tiles, LANES), jnp.float32),
            pltpu.VMEM((3, GX, 2 * LANES), jnp.float32),
            pltpu.VMEM((3, LANES, 2 * LANES), jnp.float32),
            pltpu.VMEM((2, passes, tiles, LANES), jnp.float32),
            pltpu.VMEM((2, tiles, tiles, LANES), jnp.float32),
            pltpu.VMEM((tiles * passes, 1, LANES), jnp.float32),
            pltpu.SemaphoreType.DMA((2,)),
            pltpu.SemaphoreType.DMA((2, 2)),
            pltpu.SemaphoreType.DMA((2, 2)),
            pltpu.SemaphoreType.DMA((2,)),
        ],
        compiler_params=pltpu.CompilerParams(
            collective_id=0, has_side_effects=True, vmem_limit_bytes=40 * 2**20
        ),
    )(
        obs_local.transpose(1, 0, 2),
        obs_value.reshape(1, points),
        obs_weight.reshape(1, points),
        seg_tiles.T,
        comp_scale.reshape(1, -1),
        comp_orient.reshape(1, -1),
        comp_place.reshape(1, -1),
    )
    coefficients, field = pl.pallas_call(
        hand_over,
        out_shape=(
            jax.ShapeDtypeStruct((1, LANES), jnp.float32),
            jax.ShapeDtypeStruct((8, LANES), jnp.float32),
        ),
        in_specs=[vmem, vmem],
        out_specs=(hbm, hbm),
        scratch_shapes=[pltpu.SemaphoreType.DMA((2,))],
    )(coefficients, field)
    return coefficients.reshape(-1), field.reshape(1, 1, GX * GY)


def solution(mesh):
    return jax.shard_map(
        functools.partial(on_device, mesh.shape["tile"], mesh.shape["pass"]),
        mesh=mesh,
        in_specs=(
            P(None, None, ("tile", "pass")),
            P(("tile", "pass")),
            P(("tile", "pass")),
            P(("tile", "pass"), None),
            P("tile"),
            P("tile"),
            P("tile"),
        ),
        out_specs=(P("tile"), P("tile", "pass", None)),
        check_vma=False,
    )
```

```python
import functools
import math

import jax
import jax.numpy as jnp
import numpy as np
from jax import lax
from jax.experimental import pallas as pl
from jax.experimental.pallas import tpu as pltpu
from jax.sharding import PartitionSpec as P

GX = 32
GY = 32
LANES = 128
TIME_RATE = 8.0
TIME_SCALE = math.sqrt(TIME_RATE)
MESH = pl.DeviceIdType.MESH


def cosine_polynomial(degree):
    fit = np.polynomial.Chebyshev.interpolate(
        lambda z: np.cos(2 * np.pi * np.sqrt(np.maximum(z, 0.0))), degree, domain=[0.0, 0.25]
    )
    return [float(c) for c in fit.convert(kind=np.polynomial.Polynomial).coef]


COSINE = cosine_polynomial(6)


def cos_turns(turns):
    part = turns - jnp.round(turns)
    square = part * part
    total = jnp.full_like(square, COSINE[-1])
    for coefficient in COSINE[-2::-1]:
        total = total * square + coefficient
    return total


def peers(count, body):
    if count <= 32:
        for distance in range(1, count):
            body(distance)
    else:

        def step(distance, carry):
            body(distance)
            return carry

        lax.fori_loop(1, count, step, 0)


def split(value):
    high = value.astype(jnp.bfloat16)
    return high, (value - high.astype(jnp.float32)).astype(jnp.bfloat16)


def total_of(value):
    return jnp.sum(jnp.sum(value, axis=1, keepdims=True), axis=0, keepdims=True)


def kernel(
    tiles, passes, obs_in, value_in, weight_in, seg_in, scale_in, orient_in, place_in,
    coef_ref, field_ref,
    obs_ref, value_ref, weight_ref, seg_ref, scale_ref, orient_ref, place_ref, input_sems,
    table, stack, wide, basis, vectors, grid_x, grid_y,
    near, far, last, table_sems, near_sems, far_sems, last_sems,
):
    my_tile, my_pass = lax.axis_index("tile"), lax.axis_index("pass")
    fan_out, seg_count = seg_ref.shape
    points = value_ref.shape[1]
    seg_length = points // seg_count

    barrier = pltpu.get_barrier_semaphore()
    peers(passes, lambda d: pl.semaphore_signal(
        barrier, inc=1, device_id={"pass": lax.rem(my_pass + d, passes)}, device_id_type=MESH))
    peers(tiles, lambda d: pl.semaphore_signal(
        barrier, inc=1, device_id={"tile": lax.rem(my_tile + d, tiles)}, device_id_type=MESH))

    inputs = [
        pltpu.make_async_copy(source, target, input_sems.at[place])
        for place, (source, target) in enumerate((
            (scale_in, scale_ref), (orient_in, orient_ref), (place_in, place_ref),
            (obs_in, obs_ref), (value_in, value_ref), (weight_in, weight_ref), (seg_in, seg_ref),
        ))
    ]
    for copy in inputs:
        copy.start()

    def to_peer(buffer, axis, me, count, sems, distance):
        return pltpu.make_async_remote_copy(
            src_ref=buffer.at[me],
            dst_ref=buffer.at[me],
            send_sem=sems.at[0],
            recv_sem=sems.at[1],
            device_id={axis: lax.rem(me + distance, count)},
            device_id_type=MESH,
        )

    for copy in inputs[:3]:
        copy.wait()
    def wait_for_peers(buffer, count, sem):
        slots = buffer.at[pl.ds(0, count - 1)]
        pltpu.make_async_copy(slots, slots, sem).wait()

    level = scale_ref[...].astype(jnp.float32)
    width = 0.4 * jnp.exp(level * math.log(0.7))
    wave = 2.2 / (2.0 * math.pi) / width
    turns = orient_ref[...].astype(jnp.float32) / 16.0
    place = place_ref[...]
    table[my_tile, 0:1, :] = ((place & 7).astype(jnp.float32) + 0.5) / 8.0
    table[my_tile, 1:2, :] = (((place >> 3) & 7).astype(jnp.float32) + 0.5) / 8.0
    table[my_tile, 2:3, :] = ((place >> 6).astype(jnp.float32) + 0.5) * (TIME_SCALE / 8.0)
    table[my_tile, 3:4, :] = 0.5 / (width * width)
    table[my_tile, 4:5, :] = wave * cos_turns(turns)
    table[my_tile, 5:6, :] = wave * cos_turns(turns - 0.25)
    table[my_tile, 6:7, :] = 2.0 * jnp.exp(level * math.log(1.5))
    table[my_tile, 7:8, :] = jnp.zeros((1, LANES), jnp.float32)

    pl.semaphore_wait(barrier, passes + tiles - 2)
    peers(tiles, lambda d: to_peer(table, "tile", my_tile, tiles, table_sems, d).start())

    for copy in inputs[3:]:
        copy.wait()
    roots = jnp.sqrt(weight_ref[...])
    for route in range(fan_out):
        for axis in range(3):
            line = obs_ref[axis, route : route + 1, :]
            row = 3 * route + axis
            stack[row : row + 1, :] = line * TIME_SCALE if axis == 2 else line
    root_row, value_row = 3 * fan_out, 3 * fan_out + 1
    stack[root_row : root_row + 1, :] = roots
    stack[value_row : value_row + 1, :] = roots * value_ref[...]

    def widen(block, carry):
        start = pl.multiple_of(block * LANES, LANES)
        columns = stack[:, pl.ds(start, LANES)].T
        for which in range(value_row + 1):
            wide[which, pl.ds(start, LANES), :] = jnp.broadcast_to(
                columns[:, which : which + 1], (LANES, LANES)
            )
        return carry

    lax.fori_loop(0, points // LANES, widen, 0, unroll=4)

    def column(seg, which):
        return wide[which, pl.ds(pl.multiple_of(seg * seg_length, seg_length), seg_length), :]

    wait_for_peers(table, tiles, table_sems.at[1])

    tile_row = lax.broadcasted_iota(jnp.int32, (tiles, LANES), 0)

    def gather_into(running, tile, block):
        part = jnp.sum(block, axis=0, keepdims=True)
        return running + jnp.where(tile_row == tile, part, 0.0)

    def build(seg, running):
        root, weighted = column(seg, root_row), column(seg, value_row)
        for route in range(fan_out):
            tile = seg_ref[route, seg]
            param = lambda row: table[tile, row : row + 1, :]
            delta_x = column(seg, 3 * route) - param(0)
            delta_y = column(seg, 3 * route + 1) - param(1)
            delta_t = column(seg, 3 * route + 2) - param(2)
            envelope = jnp.exp(
                -(delta_x * delta_x + delta_y * delta_y) * param(3) - delta_t * delta_t
            )
            phi = envelope * root * cos_turns(delta_x * param(4) + delta_y * param(5))
            basis[seg * fan_out + route] = phi
            running = gather_into(running, tile, phi * weighted)
        return running

    def forward(which, seg):
        total = jnp.zeros((seg_length, LANES), jnp.float32)
        for route in range(fan_out):
            tile = seg_ref[route, seg]
            total = total + basis[seg * fan_out + route] * vectors[which, pl.ds(tile, 1), :]
        return jnp.sum(total, axis=1, keepdims=True)

    def normal(seg, running):
        weighted = forward(0, seg)
        for route in range(fan_out):
            running = gather_into(
                running, seg_ref[route, seg], basis[seg * fan_out + route] * weighted
            )
        return running

    def energy(seg, running):
        values = forward(1, seg)
        return running + values * values

    def sum_slots(buffer, count):
        if count <= 8:
            total = buffer[0]
            for slot in range(1, count):
                total = total + buffer[slot]
            return total
        return lax.fori_loop(1, count, lambda slot, total: total + buffer[slot], buffer[0])

    def all_sum(value, near_slots, far_slots, near_sem, far_sem, beside=None):
        near_slots[my_pass] = value
        peers(passes, lambda d: to_peer(near_slots, "pass", my_pass, passes, near_sem, d).start())
        if beside is not None:
            beside[0]()
        wait_for_peers(near_slots, passes, near_sem.at[1])
        far_slots[my_tile] = sum_slots(near_slots, passes)
        peers(tiles, lambda d: to_peer(far_slots, "tile", my_tile, tiles, far_sem, d).start())
        if beside is not None:
            beside[1]()
        wait_for_peers(far_slots, tiles, far_sem.at[1])
        return sum_slots(far_slots, tiles)

    def grid_params(neighbor):
        tile = lax.rem(my_tile + (neighbor - 1) + tiles, tiles)
        return tile, lambda row: table[tile, row : row + 1, :]

    def axis_factors(delta, inverse, wave_row):
        envelope = jnp.exp(-(delta * delta) * inverse)
        phase = delta * wave_row
        return envelope * cos_turns(phase), envelope * cos_turns(phase - 0.25)

    def grid_factors_y():
        cell = lax.broadcasted_iota(jnp.int32, (LANES, LANES), 0) & (GY - 1)
        place_y = (cell.astype(jnp.float32) + 0.5) / GY

        def one(neighbor, carry):
            _, param = grid_params(neighbor)
            even, odd = axis_factors(place_y - param(1), param(3), param(5))
            for half, factor in enumerate((even, odd)):
                high, low = split(factor)
                grid_y[neighbor, 0, :, half * LANES : half * LANES + LANES] = high
                grid_y[neighbor, 1, :, half * LANES : half * LANES + LANES] = low
            return carry

        lax.fori_loop(0, 3, one, 0)

    def grid_factors_x():
        row = lax.broadcasted_iota(jnp.int32, (GX, LANES), 0)
        cell = (row & 7) * (GX // 8) + (row >> 3)
        place_x = (cell.astype(jnp.float32) + 0.5) / GX
        day = (my_pass.astype(jnp.float32) + 0.5) / passes * TIME_SCALE

        def one(neighbor, carry):
            _, param = grid_params(neighbor)
            side = (neighbor - 1).astype(jnp.float32)
            even, odd = axis_factors(place_x - (param(0) + side), param(3), param(4))
            delta_t = day - param(2)
            in_time = jnp.exp(-(delta_t * delta_t))
            grid_x[neighbor, :, :LANES] = even * in_time
            grid_x[neighbor, :, LANES:] = -odd * in_time
            return carry

        lax.fori_loop(0, 3, one, 0)

    zeros = jnp.zeros((tiles, LANES), jnp.float32)
    rhs = all_sum(
        lax.fori_loop(0, seg_count, build, zeros, unroll=4),
        near.at[0], far.at[0], near_sems.at[0], far_sems.at[0],
        (grid_factors_x, grid_factors_y),
    )
    prior, norms = table[:, 6, :], []
    vectors[0] = rhs
    image = all_sum(
        lax.fori_loop(0, seg_count, normal, zeros, unroll=8),
        near.at[1], far.at[1], near_sems.at[1], far_sems.at[1],
        (lambda: norms.append(total_of(rhs * rhs)), lambda: None),
    ) + prior * rhs
    norm_first = norms[0]
    step_first = norm_first / total_of(rhs * image)
    residual = rhs - step_first * image
    norm_next = total_of(residual * residual)
    direction = residual + norm_next / norm_first * rhs
    vectors[1] = direction

    fields = []

    def grid_fields():
        def one(neighbor, total):
            tile, _ = grid_params(neighbor)
            parts = []
            for which in range(2):
                row = vectors[which, pl.ds(tile, 1), :]
                parts.append(grid_x[neighbor] * jnp.concatenate([row, row], axis=1))
            high, low = split(jnp.concatenate(parts, axis=0))

            def dot(left, right):
                return lax.dot_general(
                    left, right, (((1,), (1,)), ((), ())), preferred_element_type=jnp.float32
                )

            return total + (
                dot(high, grid_y[neighbor, 0])
                + (dot(high, grid_y[neighbor, 1]) + dot(low, grid_y[neighbor, 0]))
            )

        total = lax.fori_loop(0, 3, one, jnp.zeros((2 * GX, LANES), jnp.float32))
        group = lax.broadcasted_iota(jnp.int32, (8, LANES), 1) // GY
        for begin in (0, GX):
            field = jnp.zeros((8, LANES), jnp.float32)
            for part in range(GX // 8):
                field = field + jnp.where(
                    group == part, total[begin + 8 * part : begin + 8 * part + 8, :], 0.0
                )
            fields.append(field)

    energies = lax.fori_loop(
        0, seg_count, energy, jnp.zeros((seg_length, 1), jnp.float32), unroll=8
    )
    me, everyone = my_tile * passes + my_pass, tiles * passes

    def to_anyone(distance):
        other = lax.rem(me + distance, everyone)
        return pltpu.make_async_remote_copy(
            src_ref=last.at[me],
            dst_ref=last.at[me],
            send_sem=last_sems.at[0],
            recv_sem=last_sems.at[1],
            device_id={"tile": other // passes, "pass": lax.rem(other, passes)},
            device_id_type=MESH,
        )

    last[me] = jnp.broadcast_to(jnp.sum(energies, axis=0, keepdims=True), (1, LANES))
    peers(everyone, lambda d: to_anyone(d).start())
    grid_fields()
    prior_product = total_of(direction * direction * prior)
    wait_for_peers(last, everyone, last_sems.at[1])
    product = jnp.sum(last[:, 0, :], axis=0, keepdims=True)[:, 0:1] + prior_product
    step_second = norm_next / product
    mine = pl.ds(my_tile, 1)
    coef_ref[...] = step_first * vectors[0, mine, :] + step_second * vectors[1, mine, :]
    field_ref[...] = step_first * fields[0] + step_second * fields[1]

    wait_for_peers(table, tiles, table_sems.at[0])
    for stage in range(2):
        wait_for_peers(near.at[stage], passes, near_sems.at[stage, 0])
        wait_for_peers(far.at[stage], tiles, far_sems.at[stage, 0])
    wait_for_peers(last, everyone, last_sems.at[0])


def hand_over(coef_in, field_in, coef_ref, field_ref, sems):
    copies = [
        pltpu.make_async_copy(coef_in, coef_ref, sems.at[0]),
        pltpu.make_async_copy(field_in, field_ref, sems.at[1]),
    ]
    for copy in copies:
        copy.start()
    for copy in copies:
        copy.wait()


def on_device(tiles, passes, obs_local, obs_value, obs_weight, seg_tiles, comp_scale, comp_orient, comp_place):
    seg_count, fan_out = seg_tiles.shape
    points = obs_value.shape[0]
    seg_length = points // seg_count
    vmem = pl.BlockSpec(memory_space=pltpu.VMEM)
    coefficients, field = pl.pallas_call(
        functools.partial(kernel, tiles, passes),
        out_shape=(
            jax.ShapeDtypeStruct((1, LANES), jnp.float32),
            jax.ShapeDtypeStruct((8, LANES), jnp.float32),
        ),
        in_specs=[pl.BlockSpec(memory_space=pl.ANY)] * 7,
        out_specs=(vmem, vmem),
        scratch_shapes=[
            pltpu.VMEM((3, fan_out, points), jnp.float32),
            pltpu.VMEM((1, points), jnp.float32),
            pltpu.VMEM((1, points), jnp.float32),
            pltpu.SMEM((fan_out, seg_count), jnp.int32),
            pltpu.VMEM((1, LANES), jnp.int32),
            pltpu.VMEM((1, LANES), jnp.int32),
            pltpu.VMEM((1, LANES), jnp.int32),
            pltpu.SemaphoreType.DMA((7,)),
            pltpu.VMEM((tiles, 8, LANES), jnp.float32),
            pltpu.VMEM((3 * fan_out + 2, points), jnp.float32),
            pltpu.VMEM((3 * fan_out + 2, points, LANES), jnp.float32),
            pltpu.VMEM((seg_count * fan_out, seg_length, LANES), jnp.float32),
            pltpu.VMEM((2, tiles, LANES), jnp.float32),
            pltpu.VMEM((3, GX, 2 * LANES), jnp.float32),
            pltpu.VMEM((3, 2, LANES, 2 * LANES), jnp.bfloat16),
            pltpu.VMEM((2, passes, tiles, LANES), jnp.float32),
            pltpu.VMEM((2, tiles, tiles, LANES), jnp.float32),
            pltpu.VMEM((tiles * passes, 1, LANES), jnp.float32),
            pltpu.SemaphoreType.DMA((2,)),
            pltpu.SemaphoreType.DMA((2, 2)),
            pltpu.SemaphoreType.DMA((2, 2)),
            pltpu.SemaphoreType.DMA((2,)),
        ],
        compiler_params=pltpu.CompilerParams(
            collective_id=0, has_side_effects=True, vmem_limit_bytes=60 * 2**20
        ),
    )(
        obs_local.transpose(1, 0, 2),
        obs_value.reshape(1, points),
        obs_weight.reshape(1, points),
        seg_tiles.T,
        comp_scale.reshape(1, -1),
        comp_orient.reshape(1, -1),
        comp_place.reshape(1, -1),
    )
    anywhere = pl.BlockSpec(memory_space=pl.ANY)
    coefficients, field = pl.pallas_call(
        hand_over,
        out_shape=(
            jax.ShapeDtypeStruct((1, LANES), jnp.float32),
            jax.ShapeDtypeStruct((8, LANES), jnp.float32),
        ),
        in_specs=[anywhere, anywhere],
        out_specs=(anywhere, anywhere),
        scratch_shapes=[pltpu.SemaphoreType.DMA((2,))],
        compiler_params=pltpu.CompilerParams(vmem_limit_bytes=60 * 2**20),
    )(coefficients, field)
    return coefficients.reshape(-1), field.reshape(1, 1, GX * GY)


def solution(mesh):
    return jax.shard_map(
        functools.partial(on_device, mesh.shape["tile"], mesh.shape["pass"]),
        mesh=mesh,
        in_specs=(
            P(None, None, ("tile", "pass")),
            P(("tile", "pass")),
            P(("tile", "pass")),
            P(("tile", "pass"), None),
            P("tile"),
            P("tile"),
            P("tile"),
        ),
        out_specs=(P("tile"), P("tile", "pass", None)),
        check_vma=False,
    )
```

```python
import functools
import math

import jax
import jax.numpy as jnp
import numpy as np
from jax import lax
from jax.experimental import pallas as pl
from jax.experimental.pallas import tpu as pltpu
from jax.sharding import PartitionSpec as P

GX = 32
GY = 32
LANES = 128
TIME_RATE = 8.0
LOG2E = math.log2(math.e)
TIME_SCALE = math.sqrt(TIME_RATE * LOG2E)
HIGHEST = lax.Precision.HIGHEST
MESH = pl.DeviceIdType.MESH


def cosine_polynomial(degree):
    fit = np.polynomial.Chebyshev.interpolate(
        lambda z: np.cos(2 * np.pi * np.sqrt(np.maximum(z, 0.0))), degree, domain=[0.0, 0.25]
    )
    return [float(c) for c in fit.convert(kind=np.polynomial.Polynomial).coef]


COSINE = cosine_polynomial(6)


def cos_turns(turns):
    part = turns - jnp.round(turns)
    square = part * part
    total = jnp.full_like(square, COSINE[-1])
    for coefficient in COSINE[-2::-1]:
        total = total * square + coefficient
    return total


def peers(count, body):
    if count <= 32:
        for distance in range(1, count):
            body(distance)
    else:

        def step(distance, carry):
            body(distance)
            return carry

        lax.fori_loop(1, count, step, 0)


def total_of(value):
    return jnp.sum(jnp.sum(value, axis=1, keepdims=True), axis=0, keepdims=True)


def kernel(
    tiles, passes, obs_in, value_in, weight_in, seg_in, scale_in, orient_in, place_in,
    coef_ref, field_ref,
    obs_ref, value_ref, weight_ref, seg_ref, scale_ref, orient_ref, place_ref, input_sems,
    table, stack, wide, basis, vectors, grid_x, grid_y,
    near, far, last_near, last_far, table_sems, near_sems, far_sems,
):
    my_tile, my_pass = lax.axis_index("tile"), lax.axis_index("pass")
    fan_out, seg_count = seg_ref.shape
    points = value_ref.shape[1]
    seg_length = points // seg_count

    inputs = [
        pltpu.make_async_copy(source, target, input_sems.at[place])
        for place, (source, target) in enumerate((
            (scale_in, scale_ref), (orient_in, orient_ref), (place_in, place_ref),
            (obs_in, obs_ref), (value_in, value_ref), (weight_in, weight_ref), (seg_in, seg_ref),
        ))
    ]
    for copy in inputs:
        copy.start()

    barrier = pltpu.get_barrier_semaphore()
    peers(passes, lambda d: pl.semaphore_signal(
        barrier, inc=1, device_id={"pass": lax.rem(my_pass + d, passes)}, device_id_type=MESH))
    peers(tiles, lambda d: pl.semaphore_signal(
        barrier, inc=1, device_id={"tile": lax.rem(my_tile + d, tiles)}, device_id_type=MESH))

    def to_peer(buffer, axis, me, count, sems, distance):
        return pltpu.make_async_remote_copy(
            src_ref=buffer.at[me],
            dst_ref=buffer.at[me],
            send_sem=sems.at[0],
            recv_sem=sems.at[1],
            device_id={axis: lax.rem(me + distance, count)},
            device_id_type=MESH,
        )

    for copy in inputs[:3]:
        copy.wait()
    def wait_for_peers(buffer, count, sem):
        slots = buffer.at[pl.ds(0, count - 1)]
        pltpu.make_async_copy(slots, slots, sem).wait()

    level = scale_ref[...].astype(jnp.float32)
    width = 0.4 * jnp.exp(level * math.log(0.7))
    wave = 2.2 / (2.0 * math.pi) / width
    turns = orient_ref[...].astype(jnp.float32) / 16.0
    place = place_ref[...]
    table[my_tile, 0:1, :] = ((place & 7).astype(jnp.float32) + 0.5) / 8.0
    table[my_tile, 1:2, :] = (((place >> 3) & 7).astype(jnp.float32) + 0.5) / 8.0
    table[my_tile, 2:3, :] = ((place >> 6).astype(jnp.float32) + 0.5) * (TIME_SCALE / 8.0)
    table[my_tile, 3:4, :] = 0.5 * LOG2E / (width * width)
    table[my_tile, 4:5, :] = wave * cos_turns(turns)
    table[my_tile, 5:6, :] = wave * cos_turns(turns - 0.25)
    table[my_tile, 6:7, :] = 2.0 * jnp.exp(level * math.log(1.5))
    table[my_tile, 7:8, :] = jnp.zeros((1, LANES), jnp.float32)

    pl.semaphore_wait(barrier, passes + tiles - 2)
    peers(tiles, lambda d: to_peer(table, "tile", my_tile, tiles, table_sems, d).start())

    for copy in inputs[3:]:
        copy.wait()
    roots = jnp.sqrt(weight_ref[...])
    for route in range(fan_out):
        for axis in range(3):
            line = obs_ref[axis, route : route + 1, :]
            row = 3 * route + axis
            stack[row : row + 1, :] = line * TIME_SCALE if axis == 2 else line
    root_row, value_row = 3 * fan_out, 3 * fan_out + 1
    stack[root_row : root_row + 1, :] = roots
    stack[value_row : value_row + 1, :] = roots * value_ref[...]

    def widen(block, carry):
        start = pl.multiple_of(block * LANES, LANES)
        columns = stack[:, pl.ds(start, LANES)].T
        for which in range(value_row + 1):
            wide[which, pl.ds(start, LANES), :] = jnp.broadcast_to(
                columns[:, which : which + 1], (LANES, LANES)
            )
        return carry

    lax.fori_loop(0, points // LANES, widen, 0, unroll=4)

    def column(seg, which):
        return wide[which, pl.ds(pl.multiple_of(seg * seg_length, seg_length), seg_length), :]

    wait_for_peers(table, tiles, table_sems.at[1])

    tile_row = lax.broadcasted_iota(jnp.int32, (tiles, LANES), 0)

    def gather_into(running, tile, block):
        part = jnp.sum(block, axis=0, keepdims=True)
        return running + jnp.where(tile_row == tile, part, 0.0)

    def build(seg, running):
        root, weighted = column(seg, root_row), column(seg, value_row)
        for route in range(fan_out):
            tile = seg_ref[route, seg]
            param = lambda row: table[tile, row : row + 1, :]
            delta_x = column(seg, 3 * route) - param(0)
            delta_y = column(seg, 3 * route + 1) - param(1)
            delta_t = column(seg, 3 * route + 2) - param(2)
            envelope = jnp.exp2(
                -(delta_x * delta_x + delta_y * delta_y) * param(3) - delta_t * delta_t
            )
            phi = envelope * root * cos_turns(delta_x * param(4) + delta_y * param(5))
            basis[seg * fan_out + route] = phi
            running = gather_into(running, tile, phi * weighted)
        return running

    def forward(which, seg):
        total = jnp.zeros((seg_length, LANES), jnp.float32)
        for route in range(fan_out):
            tile = seg_ref[route, seg]
            total = total + basis[seg * fan_out + route] * vectors[which, pl.ds(tile, 1), :]
        return jnp.sum(total, axis=1, keepdims=True)

    def normal(seg, running):
        weighted = forward(0, seg)
        for route in range(fan_out):
            running = gather_into(
                running, seg_ref[route, seg], basis[seg * fan_out + route] * weighted
            )
        return running

    def energy(seg, running):
        values = forward(1, seg)
        return running + values * values

    def sum_slots(buffer, count):
        if count <= 8:
            total = buffer[0]
            for slot in range(1, count):
                total = total + buffer[slot]
            return total
        return lax.fori_loop(1, count, lambda slot, total: total + buffer[slot], buffer[0])

    def all_sum(value, near_slots, far_slots, near_sem, far_sem, beside=None):
        near_slots[my_pass] = value
        peers(passes, lambda d: to_peer(near_slots, "pass", my_pass, passes, near_sem, d).start())
        if beside is not None:
            beside[0]()
        wait_for_peers(near_slots, passes, near_sem.at[1])
        far_slots[my_tile] = sum_slots(near_slots, passes)
        peers(tiles, lambda d: to_peer(far_slots, "tile", my_tile, tiles, far_sem, d).start())
        if beside is not None:
            beside[1]()
        wait_for_peers(far_slots, tiles, far_sem.at[1])
        return sum_slots(far_slots, tiles)

    def grid_params(neighbor):
        tile = lax.rem(my_tile + (neighbor - 1) + tiles, tiles)
        return tile, lambda row: table[tile, row : row + 1, :]

    def axis_factors(delta, inverse, wave_row):
        envelope = jnp.exp2(-(delta * delta) * inverse)
        phase = delta * wave_row
        return envelope * cos_turns(phase), envelope * cos_turns(phase - 0.25)

    def grid_factors_y():
        cell = lax.broadcasted_iota(jnp.int32, (LANES, LANES), 0) & (GY - 1)
        place_y = (cell.astype(jnp.float32) + 0.5) / GY
        for neighbor in range(3):
            _, param = grid_params(neighbor)
            even, odd = axis_factors(place_y - param(1), param(3), param(5))
            grid_y[neighbor, :, :LANES] = even
            grid_y[neighbor, :, LANES:] = odd

    def grid_factors_x():
        row = lax.broadcasted_iota(jnp.int32, (GX, LANES), 0)
        cell = (row & 7) * (GX // 8) + (row >> 3)
        place_x = (cell.astype(jnp.float32) + 0.5) / GX
        day = (my_pass.astype(jnp.float32) + 0.5) / passes * TIME_SCALE
        for neighbor in range(3):
            _, param = grid_params(neighbor)
            even, odd = axis_factors(
                place_x - (param(0) + float(neighbor - 1)), param(3), param(4)
            )
            delta_t = day - param(2)
            in_time = jnp.exp2(-(delta_t * delta_t))
            grid_x[neighbor, :, :LANES] = even * in_time
            grid_x[neighbor, :, LANES:] = -odd * in_time

    zeros = jnp.zeros((tiles, LANES), jnp.float32)
    rhs = all_sum(
        lax.fori_loop(0, seg_count, build, zeros, unroll=4),
        near.at[0], far.at[0], near_sems.at[0], far_sems.at[0],
        (grid_factors_x, grid_factors_y),
    )
    prior, norms = table[:, 6, :], []
    vectors[0] = rhs
    image = all_sum(
        lax.fori_loop(0, seg_count, normal, zeros, unroll=8),
        near.at[1], far.at[1], near_sems.at[1], far_sems.at[1],
        (lambda: norms.append(total_of(rhs * rhs)), lambda: None),
    ) + prior * rhs
    norm_first = norms[0]
    step_first = norm_first / total_of(rhs * image)
    residual = rhs - step_first * image
    norm_next = total_of(residual * residual)
    direction = residual + norm_next / norm_first * rhs
    vectors[1] = direction

    fields = []

    def grid_fields():
        total = None
        for neighbor in range(3):
            tile, _ = grid_params(neighbor)
            parts = []
            for which in range(2):
                row = vectors[which, pl.ds(tile, 1), :]
                parts.append(grid_x[neighbor] * jnp.concatenate([row, row], axis=1))
            term = lax.dot_general(
                jnp.concatenate(parts, axis=0),
                grid_y[neighbor],
                (((1,), (1,)), ((), ())),
                precision=HIGHEST,
                preferred_element_type=jnp.float32,
            )
            total = term if total is None else total + term
        group = lax.broadcasted_iota(jnp.int32, (8, LANES), 1) // GY
        for begin in (0, GX):
            field = jnp.zeros((8, LANES), jnp.float32)
            for part in range(GX // 8):
                field = field + jnp.where(
                    group == part, total[begin + 8 * part : begin + 8 * part + 8, :], 0.0
                )
            fields.append(field)

    energies = lax.fori_loop(
        0, seg_count, energy, jnp.zeros((seg_length, 1), jnp.float32), unroll=8
    )
    parts = []
    product = all_sum(
        jnp.broadcast_to(jnp.sum(energies, axis=0, keepdims=True), (1, LANES)),
        last_near, last_far, near_sems.at[2], far_sems.at[2],
        (lambda: parts.append(total_of(direction * direction * prior)), grid_fields),
    )[:, 0:1] + parts[0]
    step_second = norm_next / product
    mine = pl.ds(my_tile, 1)
    coef_ref[...] = step_first * vectors[0, mine, :] + step_second * vectors[1, mine, :]
    field_ref[...] = step_first * fields[0] + step_second * fields[1]

    wait_for_peers(table, tiles, table_sems.at[0])
    for stage in range(2):
        wait_for_peers(near.at[stage], passes, near_sems.at[stage, 0])
        wait_for_peers(far.at[stage], tiles, far_sems.at[stage, 0])
    wait_for_peers(last_near, passes, near_sems.at[2, 0])
    wait_for_peers(last_far, tiles, far_sems.at[2, 0])


def hand_over(coef_in, field_in, coef_ref, field_ref, sems):
    copies = [
        pltpu.make_async_copy(coef_in, coef_ref, sems.at[0]),
        pltpu.make_async_copy(field_in, field_ref, sems.at[1]),
    ]
    for copy in copies:
        copy.start()
    for copy in copies:
        copy.wait()


def on_device(tiles, passes, obs_local, obs_value, obs_weight, seg_tiles, comp_scale, comp_orient, comp_place):
    seg_count, fan_out = seg_tiles.shape
    points = obs_value.shape[0]
    seg_length = points // seg_count
    vmem = pl.BlockSpec(memory_space=pltpu.VMEM)
    coefficients, field = pl.pallas_call(
        functools.partial(kernel, tiles, passes),
        out_shape=(
            jax.ShapeDtypeStruct((1, LANES), jnp.float32),
            jax.ShapeDtypeStruct((8, LANES), jnp.float32),
        ),
        in_specs=[pl.BlockSpec(memory_space=pl.ANY)] * 7,
        out_specs=(vmem, vmem),
        scratch_shapes=[
            pltpu.VMEM((3, fan_out, points), jnp.float32),
            pltpu.VMEM((1, points), jnp.float32),
            pltpu.VMEM((1, points), jnp.float32),
            pltpu.SMEM((fan_out, seg_count), jnp.int32),
            pltpu.VMEM((1, LANES), jnp.int32),
            pltpu.VMEM((1, LANES), jnp.int32),
            pltpu.VMEM((1, LANES), jnp.int32),
            pltpu.SemaphoreType.DMA((7,)),
            pltpu.VMEM((tiles, 8, LANES), jnp.float32),
            pltpu.VMEM((3 * fan_out + 2, points), jnp.float32),
            pltpu.VMEM((3 * fan_out + 2, points, LANES), jnp.float32),
            pltpu.VMEM((seg_count * fan_out, seg_length, LANES), jnp.float32),
            pltpu.VMEM((2, tiles, LANES), jnp.float32),
            pltpu.VMEM((3, GX, 2 * LANES), jnp.float32),
            pltpu.VMEM((3, LANES, 2 * LANES), jnp.float32),
            pltpu.VMEM((2, passes, tiles, LANES), jnp.float32),
            pltpu.VMEM((2, tiles, tiles, LANES), jnp.float32),
            pltpu.VMEM((passes, 1, LANES), jnp.float32),
            pltpu.VMEM((tiles, 1, LANES), jnp.float32),
            pltpu.SemaphoreType.DMA((2,)),
            pltpu.SemaphoreType.DMA((3, 2)),
            pltpu.SemaphoreType.DMA((3, 2)),
        ],
        compiler_params=pltpu.CompilerParams(
            collective_id=0, has_side_effects=True, vmem_limit_bytes=60 * 2**20
        ),
    )(
        obs_local.transpose(1, 0, 2),
        obs_value.reshape(1, points),
        obs_weight.reshape(1, points),
        seg_tiles.T,
        comp_scale.reshape(1, -1),
        comp_orient.reshape(1, -1),
        comp_place.reshape(1, -1),
    )
    anywhere = pl.BlockSpec(memory_space=pl.ANY)
    coefficients, field = pl.pallas_call(
        hand_over,
        out_shape=(
            jax.ShapeDtypeStruct((1, LANES), jnp.float32),
            jax.ShapeDtypeStruct((8, LANES), jnp.float32),
        ),
        in_specs=[anywhere, anywhere],
        out_specs=(anywhere, anywhere),
        scratch_shapes=[pltpu.SemaphoreType.DMA((2,))],
        compiler_params=pltpu.CompilerParams(vmem_limit_bytes=60 * 2**20),
    )(coefficients, field)
    return coefficients.reshape(-1), field.reshape(1, 1, GX * GY)


def solution(mesh):
    return jax.shard_map(
        functools.partial(on_device, mesh.shape["tile"], mesh.shape["pass"]),
        mesh=mesh,
        in_specs=(
            P(None, None, ("tile", "pass")),
            P(("tile", "pass")),
            P(("tile", "pass")),
            P(("tile", "pass"), None),
            P("tile"),
            P("tile"),
            P("tile"),
        ),
        out_specs=(P("tile"), P("tile", "pass", None)),
        check_vma=False,
    )
```
